256 devices in a mesh: row: 8 (over x, y_hi), col: 32 (over z, y_lo, core).
Axes of the slice: x: 4, y: 4 (y_hi: 2, y_lo: 2; y = y_hi * 2 + y_lo), z: 8, core: 2. Of those that a mesh axis runs over, the one named last changes fastest.
Arguments:
- latent: bfloat16 [8192, 1280], P(('row', 'col')), may hold values from -26 to 26
- gn_gain: float32 [1280], replicated, may hold values from 0.25 to 1.75
- gn_bias: float32 [1280], replicated, may hold values from -3 to 3
- w_in: bfloat16 [1280, 1280], replicated, may hold values from -0.15625 to 0.15625
- b_in: float32 [1280], replicated, may hold values from -3 to 3
- ln_gain: float32 [1280], replicated, may hold values from 0.25 to 1.75
- ln_bias: float32 [1280], replicated, may hold values from -2 to 2
- w_query: bfloat16 [1280, 640], replicated, may hold values from -0.15625 to 0.15625
- w_key: bfloat16 [1280, 640], replicated, may hold values from -0.15625 to 0.15625
- w_value: bfloat16 [1280, 640], replicated, may hold values from -0.15625 to 0.15625
- stale_kv: bfloat16 [2, 8192, 640], P(None, ('row', 'col')), may hold values from -10 to 10
Outputs:
- stream: bfloat16 [8192, 1280], P(('row', 'col'))
- fresh_kv: bfloat16 [2, 8192, 640], P(None, ('row', 'col'))
- attended: bfloat16 [8192, 640], P(('row', 'col'))
The draws below stay inside these ranges and needn't reach their ends.
All inputs are finite; a program needn't handle non-finite values.
Results may differ from the reference program's by a relative error of at most 0.019.
Values may be sent and summed in bfloat16 or wider, within the bound.
No kernel may reach another device: no remote copies, remote signals or barrier semaphores. Data moves between devices by JAX's collectives and lax.ppermute only.
A program may use at most 128 MiB of HBM per device.

```python
import math
import jax
import jax.numpy as jnp
from jax import lax

CHANNELS = 1280
GROUPS = 32
HEADS = 10
HEAD_DIM = 64
TOK_DEV = 32
TOKENS = 8192


def draw_latent(key, part):
    key = jax.random.fold_in(key, 11)
    key_centre, key_rough, key_noise = jax.random.split(key, 3)
    place = (jnp.arange(TOKENS, dtype=jnp.float32) / TOKENS)[:, None]
    centre = jax.random.uniform(key_centre, (1, CHANNELS), jnp.float32, -1.0, 1.0)
    rough = jnp.exp(jax.random.uniform(key_rough, (TOKENS, 1), jnp.float32, -0.5, 0.5))
    noise = jax.random.truncated_normal(key_noise, -4.0, 4.0, (TOKENS, CHANNELS), jnp.float32)
    value = (1.0 + 2.0 * place) * rough * (centre + noise)
    return value.astype(jnp.bfloat16)


def block_levels(key, shape, pieces, low, largest):
    factor_of, own = 1.0, jax.random.fold_in(key, 6)
    for position, blocks in pieces:
        draws = jnp.exp(jax.random.uniform(jax.random.fold_in(own, position), (blocks,), jnp.float32, low / len(pieces), largest / len(pieces)))
        factor_of = factor_of * jnp.repeat(draws, shape[position] // blocks).reshape([-1 if axis == position else 1 for axis in range(len(shape))])
    return factor_of


def normal_values(rng, shape, deviation, most, cuts=(), held_as=jnp.bfloat16):
    values = deviation * jax.random.normal(rng, shape, jnp.float32)
    if cuts:
        values = values * block_levels(rng, shape, cuts, -0.22, 0.18)
    return jnp.clip(values, -most, most).astype(held_as)


def setup_inputs(seed: int = 0) -> dict:
    splits = jax.random.split(jax.random.key(seed), 12)
    return {
        "latent": draw_latent(jax.random.fold_in(splits[11], 71), 0),
        "gn_gain": jnp.clip(1.0 + 0.15 * jax.random.normal(splits[1], (CHANNELS,), jnp.float32), 0.25, 1.75),
        "gn_bias": normal_values(splits[2], (CHANNELS,), 0.5, 3.0, (), jnp.float32),
        "w_in": normal_values(splits[3], (CHANNELS, CHANNELS), CHANNELS ** -0.5, 0.15625),
        "b_in": normal_values(splits[4], (CHANNELS,), 0.5, 3.0, (), jnp.float32),
        "ln_gain": jnp.clip(1.0 + 0.15 * jax.random.normal(splits[5], (CHANNELS,), jnp.float32), 0.25, 1.75),
        "ln_bias": normal_values(splits[6], (CHANNELS,), 0.3, 2.0, (), jnp.float32),
        "w_query": normal_values(splits[7], (CHANNELS, HEADS * HEAD_DIM), CHANNELS ** -0.5, 0.15625),
        "w_key": normal_values(splits[8], (CHANNELS, HEADS * HEAD_DIM), CHANNELS ** -0.5, 0.15625),
        "w_value": normal_values(splits[9], (CHANNELS, HEADS * HEAD_DIM), CHANNELS ** -0.5, 0.15625),
        "stale_kv": normal_values(splits[10], (2, TOKENS, HEADS * HEAD_DIM), 2.5, 10.0, ((1, 256),)),
    }


def reference(latent, gn_gain, gn_bias, w_in, b_in, ln_gain, ln_bias, w_query, w_key, w_value, stale_kv):
    width = CHANNELS // GROUPS
    values_in = latent.astype(jnp.float32).reshape(TOKENS, GROUPS, width)
    mean = lax.optimization_barrier(jnp.mean(values_in, axis=(0, 2)))
    centred = values_in - mean[None, :, None]
    spread = lax.optimization_barrier(jnp.mean(centred * centred, axis=(0, 2)))
    scaled = (centred * lax.rsqrt(spread + 1e-06)[None, :, None]).reshape(TOKENS, CHANNELS)
    normed = (scaled * gn_gain + gn_bias).astype(jnp.bfloat16)
    stream = (jnp.dot(normed, w_in, preferred_element_type=jnp.float32) + b_in).astype(jnp.bfloat16)
    wide = stream.astype(jnp.float32)
    token_mean = lax.optimization_barrier(jnp.mean(wide, axis=-1, keepdims=True))
    token_dev = wide - token_mean
    token_var = lax.optimization_barrier(jnp.mean(token_dev * token_dev, axis=-1, keepdims=True))
    lnorm = (token_dev * lax.rsqrt(token_var + 1e-05) * ln_gain + ln_bias).astype(jnp.bfloat16)
    query = jnp.dot(lnorm, w_query, preferred_element_type=jnp.float32).astype(jnp.bfloat16)
    keys_new = jnp.dot(lnorm, w_key, preferred_element_type=jnp.float32).astype(jnp.bfloat16)
    values_new = jnp.dot(lnorm, w_value, preferred_element_type=jnp.float32).astype(jnp.bfloat16)
    fresh_kv = jnp.stack([keys_new, values_new])
    factor = 1.0 / math.sqrt(HEAD_DIM)
    patches = TOKENS // TOK_DEV

    def one_patch(index):
        start = (index * TOK_DEV).astype(jnp.int32)
        query_part = lax.dynamic_slice_in_dim(query, start, TOK_DEV, 0).astype(jnp.float32)
        query_part = query_part.reshape(TOK_DEV, HEADS, HEAD_DIM)
        own_keys = lax.dynamic_slice_in_dim(keys_new, start, TOK_DEV, 0)
        own_values = lax.dynamic_slice_in_dim(values_new, start, TOK_DEV, 0)
        all_keys = lax.dynamic_update_slice_in_dim(stale_kv[0], own_keys, start, 0)
        all_values = lax.dynamic_update_slice_in_dim(stale_kv[1], own_values, start, 0)
        all_keys = all_keys.astype(jnp.float32).reshape(TOKENS, HEADS, HEAD_DIM)
        all_values = all_values.astype(jnp.float32).reshape(TOKENS, HEADS, HEAD_DIM)
        score = jnp.einsum('qhd,khd->hqk', query_part, all_keys) * factor
        weight = jnp.exp(score)
        total = lax.optimization_barrier(jnp.sum(weight, axis=-1))
        rounded = lax.optimization_barrier(weight.astype(jnp.bfloat16)).astype(jnp.float32)
        numer = jnp.einsum('hqk,khd->qhd', rounded, all_values)
        result = numer / jnp.transpose(total)[:, :, None]
        return result.reshape(TOK_DEV, HEADS * HEAD_DIM).astype(jnp.bfloat16)
    attended = lax.map(one_patch, jnp.arange(patches, dtype=jnp.int32))
    attended = attended.reshape(TOKENS, HEADS * HEAD_DIM)
    return (stream, fresh_kv, attended)
```

```python
import math

import jax
import jax.numpy as jnp
from jax import lax
from jax.experimental import pallas as pl
from jax.experimental.pallas import tpu as pltpu
from jax.sharding import PartitionSpec as P

GROUPS = 32
HEADS = 10
HEAD_DIM = 64
AXES = ("row", "col")
DEVICES = 256
NX, NY, NZ = 4, 4, 8
Z_MASK = 0b00011100
VMEM = pl.BlockSpec(memory_space=pltpu.VMEM)
SMEM = pl.BlockSpec(memory_space=pltpu.SMEM)


def place_of(x, y, z, core):
    return x * 64 + (y // 2) * 32 + z * 4 + (y % 2) * 2 + core


def ring(dx=0, dy=0, dcore=0):
    pairs = []
    for x in range(NX):
        for y in range(NY):
            for z in range(NZ):
                for core in range(2):
                    pairs.append(
                        (
                            place_of(x, y, z, core),
                            place_of((x + dx) % NX, (y + dy) % NY, z, (core + dcore) % 2),
                        )
                    )
    return sorted(pairs)


def groups_of(mask):
    found = {}
    for i in range(DEVICES):
        found.setdefault(i & ~mask, []).append(i)
    return list(found.values())


def spread_out(value, count):
    return jnp.broadcast_to(value[None], (count,) + value.shape)


def attend_kernel(place_ref, q_ref, fresh_ref, *refs):
    key_refs, out_ref = refs[:-1], refs[-1]
    own = place_ref[0]
    rows = q_ref.shape[0]
    patch = fresh_ref.shape[1]
    lane = lax.broadcasted_iota(jnp.int32, (1, 128), 1)
    low = lane < HEAD_DIM
    row = lax.broadcasted_iota(jnp.int32, (2 * rows, 1), 0) % rows
    mine = (row >= own * patch) & (row < (own + 1) * patch)
    totals = jnp.zeros((rows, 128), jnp.float32)
    contract = (((1,), (1,)), ((), ()))
    for pair in range(HEADS // 2):
        lanes = slice(pair * 128, pair * 128 + 128)
        query = q_ref[:, lanes] * jnp.bfloat16(1.0 / math.sqrt(HEAD_DIM))
        zero = jnp.zeros_like(query)
        query = jnp.concatenate(
            [jnp.where(low, query, zero), jnp.where(low, zero, query)], axis=0
        )

        def part(keys, values, keep):
            count = keys.shape[0]
            score = lax.dot_general(query, keys, contract, preferred_element_type=jnp.float32)
            weight = jnp.exp(score)
            if keep is not None:
                weight = jnp.where(keep, weight, 0.0)
            wide = jnp.concatenate([values, jnp.ones((count, 128), jnp.bfloat16)], axis=1)
            return jnp.dot(weight.astype(jnp.bfloat16), wide, preferred_element_type=jnp.float32)

        acc = part(fresh_ref[0, :, lanes], fresh_ref[1, :, lanes], mine)
        for index, ref in enumerate(key_refs):
            count = ref.shape[0] * patch
            keep = None
            if index == 0:
                column = lax.broadcasted_iota(jnp.int32, (1, count), 1)
                keep = jnp.logical_not(mine & (column < patch))
            acc = acc + part(
                ref[:, 0, :, lanes].reshape(count, 128),
                ref[:, 1, :, lanes].reshape(count, 128),
                keep,
            )
        numer = jnp.where(low, acc[:rows, :128], acc[rows:, :128])
        out_ref[:, lanes] = numer.astype(jnp.bfloat16)
        for half in range(2):
            head = 2 * pair + half
            found = acc[half * rows : (half + 1) * rows, 128:]
            totals = jnp.where((lane == head) | (lane == 16 + head), found, totals)
    coarse = totals.astype(jnp.bfloat16)
    fine = (totals - coarse.astype(jnp.float32)).astype(jnp.bfloat16)
    out_ref[:, HEADS * HEAD_DIM :] = jnp.where(lane < 16, coarse, fine)


def attend(place, query, fresh, key_parts):
    rows = query.shape[0]
    return pl.pallas_call(
        attend_kernel,
        out_shape=jax.ShapeDtypeStruct((rows, HEADS * HEAD_DIM + 128), jnp.bfloat16),
        in_specs=[SMEM] + [VMEM] * (2 + len(key_parts)),
        out_specs=VMEM,
        compiler_params=pltpu.CompilerParams(vmem_limit_bytes=32 * 1024 * 1024),
        cost_estimate=pl.CostEstimate(
            flops=4 * rows * 1056 * HEADS * HEAD_DIM,
            bytes_accessed=3 * 1024 * 1024,
            transcendentals=rows * 1056 * HEADS,
        ),
    )(place, query, fresh, *key_parts)


def combine_kernel(parts_ref, out_ref):
    total = jnp.sum(parts_ref[:, :, HEADS * HEAD_DIM :].astype(jnp.float32), axis=0)
    low = lax.broadcasted_iota(jnp.int32, (1, 128), 1) < HEAD_DIM
    for pair in range(HEADS // 2):
        lanes = slice(pair * 128, pair * 128 + 128)
        numer = jnp.sum(parts_ref[:, :, lanes].astype(jnp.float32), axis=0)
        halves = [
            total[:, h : h + 1] + total[:, 16 + h : 17 + h] for h in (2 * pair, 2 * pair + 1)
        ]
        out_ref[:, lanes] = (numer / jnp.where(low, halves[0], halves[1])).astype(jnp.bfloat16)


def combine(parts):
    return pl.pallas_call(
        combine_kernel,
        out_shape=jax.ShapeDtypeStruct((parts.shape[1], HEADS * HEAD_DIM), jnp.bfloat16),
        in_specs=[VMEM],
        out_specs=VMEM,
    )(parts)


def local(
    latent, gn_gain, gn_bias, w_in, b_in, ln_gain, ln_bias, w_query, w_key, w_value, stale_kv
):
    rows, chans = latent.shape
    width = chans // GROUPS

    with jax.named_scope("keys_x"):
        along_x = [lax.ppermute(stale_kv, AXES, ring(dx=d)) for d in (1, 3, 2)]
        plane = jnp.stack([stale_kv] + along_x)
    with jax.named_scope("keys_y"):
        planes = [plane] + [lax.ppermute(plane, AXES, ring(dy=d)) for d in (1, 3, 2)]
    with jax.named_scope("keys_core"):
        planes = planes + [lax.ppermute(part, AXES, ring(dcore=1)) for part in planes]

    with jax.named_scope("statistics"):
        values_in = latent.astype(jnp.float32).reshape(rows, GROUPS, width)
        mean_here = jnp.mean(values_in, axis=(0, 2))
        off = values_in - mean_here[None, :, None]
        square_here = jnp.sum(off * off, axis=(0, 2))
        sent = jnp.concatenate([mean_here, square_here, jnp.zeros((64,), jnp.float32)])
        got = lax.all_to_all(spread_out(sent[None], DEVICES), AXES, 0, 0)[:, 0, :]
        means = got[:, :GROUPS]
        mean = jnp.mean(means, axis=0)
        apart = means - mean[None]
        spread = (
            jnp.sum(got[:, GROUPS : 2 * GROUPS], axis=0)
            + (rows * width) * jnp.sum(apart * apart, axis=0)
        ) / (rows * width * DEVICES)

    centred = values_in - mean[None, :, None]
    scaled = (centred * lax.rsqrt(spread + 1e-06)[None, :, None]).reshape(rows, chans)
    normed = (scaled * gn_gain + gn_bias).astype(jnp.bfloat16)
    stream = (jnp.dot(normed, w_in, preferred_element_type=jnp.float32) + b_in).astype(jnp.bfloat16)
    wide = stream.astype(jnp.float32)
    token_mean = jnp.mean(wide, axis=-1, keepdims=True)
    token_dev = wide - token_mean
    token_var = jnp.mean(token_dev * token_dev, axis=-1, keepdims=True)
    lnorm = (token_dev * lax.rsqrt(token_var + 1e-05) * ln_gain + ln_bias).astype(jnp.bfloat16)
    query = jnp.dot(lnorm, w_query, preferred_element_type=jnp.float32).astype(jnp.bfloat16)
    keys_new = jnp.dot(lnorm, w_key, preferred_element_type=jnp.float32).astype(jnp.bfloat16)
    values_new = jnp.dot(lnorm, w_value, preferred_element_type=jnp.float32).astype(jnp.bfloat16)
    fresh_kv = jnp.stack([keys_new, values_new])

    with jax.named_scope("queries"):
        queries = lax.all_to_all(
            spread_out(query, NZ), AXES, 0, 0, axis_index_groups=groups_of(Z_MASK)
        ).reshape(NZ * rows, HEADS * HEAD_DIM)
    my_z = (lax.axis_index("col") >> 2) & (NZ - 1)
    partial = attend(my_z.reshape(1).astype(jnp.int32), queries, fresh_kv, planes)
    with jax.named_scope("partials"):
        parts = lax.all_to_all(
            partial.reshape(NZ, rows, partial.shape[1]),
            AXES,
            0,
            0,
            axis_index_groups=groups_of(Z_MASK),
        )
    attended = combine(parts)
    return (stream, fresh_kv, attended)


def solution(mesh):
    placed = (
        P(AXES, None),
        P(),
        P(),
        P(),
        P(),
        P(),
        P(),
        P(),
        P(),
        P(),
        P(None, AXES, None),
    )
    return jax.shard_map(
        local,
        mesh=mesh,
        in_specs=placed,
        out_specs=(P(AXES, None), P(None, AXES, None), P(AXES, None)),
        check_vma=False,
    )
```

```python
import math
import jax
import jax.numpy as jnp
from jax import lax
from jax.experimental import pallas as pl
from jax.experimental.pallas import tpu as pltpu
from jax.sharding import PartitionSpec as P

GROUPS = 32
HEADS = 10
HEAD_DIM = 64
INNER = HEADS * HEAD_DIM
VMEM = pl.BlockSpec(memory_space=pltpu.VMEM)
SMEM = pl.BlockSpec(memory_space=pltpu.SMEM)
HBM = pl.BlockSpec(memory_space=pltpu.HBM)
NT = (((1,), (1,)), ((), ()))


def member_of(chans):
    width = chans // GROUPS
    first = lax.broadcasted_iota(jnp.int32, (chans, 128), 1) * width
    chan = lax.broadcasted_iota(jnp.int32, (chans, 128), 0)
    inside = (chan >= first) & (chan < first + width)
    return jnp.where(inside, 1.0, 0.0).astype(jnp.bfloat16)


def pieces(value):
    a = value.astype(jnp.bfloat16)
    rest = value - a.astype(jnp.float32)
    b = rest.astype(jnp.bfloat16)
    c = (rest - b.astype(jnp.float32)).astype(jnp.bfloat16)
    return jnp.concatenate([a, b, c], axis=0)


def to_groups(row, member):
    got = jnp.dot(pieces(row), member, preferred_element_type=jnp.float32)
    return got[0:1] + got[1:2] + got[2:3]


def to_channels(row, member):
    got = lax.dot_general(pieces(row), member, NT, preferred_element_type=jnp.float32)
    return got[0:1] + got[1:2] + got[2:3]


def statistics_kernel(x_ref, out_ref):
    rows, chans = x_ref.shape
    entries = rows * (chans // GROUPS)
    member = member_of(chans)
    x = x_ref[...].astype(jnp.float32)
    mean = to_groups(jnp.sum(x, axis=0, keepdims=True), member) * (1.0 / entries)
    off = x - to_channels(mean, member)
    square = to_groups(jnp.sum(off * off, axis=0, keepdims=True), member)
    lane = lax.broadcasted_iota(jnp.int32, (1, 128), 1)
    both = jnp.where(lane < GROUPS, mean, pltpu.roll(square, GROUPS, axis=1))
    out_ref[...] = jnp.broadcast_to(both, out_ref.shape)


def statistics(x, peers):
    return pl.pallas_call(
        statistics_kernel,
        out_shape=jax.ShapeDtypeStruct((peers, 128), jnp.float32),
        in_specs=[VMEM],
        out_specs=VMEM,
    )(x)


def project_kernel(stats_ref, vec_ref, x_ref, w_in_ref, w_q_hbm, stream_ref, lnorm_ref, query_ref, w_q_ref, sem):
    copy = pltpu.make_async_copy(w_q_hbm, w_q_ref, sem)
    copy.start()
    rows, chans = x_ref.shape

    peers = stats_ref.shape[0]
    entries = rows * (chans // GROUPS)
    lane = lax.broadcasted_iota(jnp.int32, (1, 128), 1)
    stats = stats_ref[...]
    sums = jnp.sum(stats, axis=0, keepdims=True)
    mean = jnp.where(lane < GROUPS, sums * (1.0 / peers), 0.0)
    apart = jnp.where(lane < GROUPS, stats - mean, 0.0)
    square = pltpu.roll(sums, 128 - GROUPS, axis=1) + entries * jnp.sum(
        apart * apart, axis=0, keepdims=True
    )
    square = jnp.where(lane < GROUPS, square, 0.0)
    member = member_of(chans)
    mean = to_channels(mean, member)
    scale = to_channels(lax.rsqrt(square * (1.0 / (entries * peers)) + 1e-06), member)

    x = x_ref[...].astype(jnp.float32)
    normed = ((x - mean) * scale * vec_ref[0:1] + vec_ref[1:2]).astype(jnp.bfloat16)
    stream = (
        jnp.dot(normed, w_in_ref[...], preferred_element_type=jnp.float32) + vec_ref[2:3]
    ).astype(jnp.bfloat16)
    stream_ref[...] = stream
    wide = stream.astype(jnp.float32)
    token_mean = jnp.mean(wide, axis=-1, keepdims=True)
    token_dev = wide - token_mean
    token_var = jnp.mean(token_dev * token_dev, axis=-1, keepdims=True)
    lnorm = token_dev * lax.rsqrt(token_var + 1e-05) * vec_ref[3:4] + vec_ref[4:5]
    lnorm = lnorm.astype(jnp.bfloat16)
    lnorm_ref[...] = lnorm
    copy.wait()
    query = jnp.dot(lnorm, w_q_ref[...], preferred_element_type=jnp.float32)
    query = query.astype(jnp.bfloat16) * jnp.bfloat16(1.0 / math.sqrt(HEAD_DIM))
    query_ref[...] = jnp.broadcast_to(query[None], query_ref.shape)


def project(stats, vectors, x, w_in, w_query, copies):
    patch, chans = x.shape
    bf16 = jnp.bfloat16
    return pl.pallas_call(
        project_kernel,
        out_shape=(
            jax.ShapeDtypeStruct((patch, chans), bf16),
            jax.ShapeDtypeStruct((patch, chans), bf16),
            jax.ShapeDtypeStruct((copies, patch, INNER), bf16),
        ),
        in_specs=[VMEM] * 4 + [HBM],
        out_specs=(VMEM, VMEM, VMEM),
        scratch_shapes=[pltpu.VMEM(w_query.shape, bf16), pltpu.SemaphoreType.DMA(())],
        compiler_params=pltpu.CompilerParams(vmem_limit_bytes=56 * 1024 * 1024),
        cost_estimate=pl.CostEstimate(
            flops=patch * 2 * chans * (chans + INNER),
            bytes_accessed=6 * 1024 * 1024,
            transcendentals=patch,
        ),
    )(stats, vectors, x, w_in, w_query)


def fresh_kernel(x_ref, w_k_ref, w_v_ref, out_ref):
    for i, w_ref in enumerate((w_k_ref, w_v_ref)):
        out_ref[i] = jnp.dot(x_ref[...], w_ref[...], preferred_element_type=jnp.float32).astype(
            jnp.bfloat16
        )


def fresh_keys(x, w_key, w_value):
    return pl.pallas_call(
        fresh_kernel,
        out_shape=jax.ShapeDtypeStruct((2, x.shape[0], INNER), jnp.bfloat16),
        in_specs=[VMEM] * 3,
        out_specs=VMEM,
        compiler_params=pltpu.CompilerParams(vmem_limit_bytes=56 * 1024 * 1024),
    )(x, w_key, w_value)


def attend_kernel(place_ref, q_ref, fresh_ref, *refs):
    sources, (out_ref, kv_ref, p_ref, sems) = refs[:-4], refs[-4:]
    copies = [
        pltpu.make_async_copy(source, kv_ref.at[i], sems.at[i])
        for i, source in enumerate(sources)
    ]
    for copy in copies:
        copy.start()
    patch = fresh_ref.shape[1]
    rows = q_ref.shape[0]
    count = rows // patch
    own = place_ref[0] * patch
    for copy in copies:
        copy.wait()
    keys = kv_ref.shape[0] * kv_ref.shape[1] * patch
    lane = lax.broadcasted_iota(jnp.int32, (1, 128), 1)
    low = lane < HEAD_DIM
    row = lax.broadcasted_iota(jnp.int32, (2 * rows, 1), 0)
    row = jnp.where(row >= rows, row - rows, row)
    is_own = (row >= own) & (row < own + patch)
    totals = jnp.zeros((rows, 128), jnp.float32)
    for pair in range(HEADS // 2):
        lanes = slice(pair * 128, pair * 128 + 128)
        part = q_ref[:, lanes]
        zero = jnp.zeros_like(part)
        part = jnp.concatenate([jnp.where(low, part, zero), jnp.where(low, zero, part)], axis=0)
        key = kv_ref[:, :, 0, :, lanes].reshape(keys, 128)
        value = kv_ref[:, :, 1, :, lanes].reshape(keys, 128)
        step = 128
        for at in range(0, keys, step):
            score = lax.dot_general(
                part, key[at : at + step], NT, preferred_element_type=jnp.float32
            )
            weight = jnp.exp(score)
            if at == 0:
                column = lax.broadcasted_iota(jnp.int32, (1, step), 1)
                weight = jnp.where(is_own & (column < patch), 0.0, weight)
            p_ref[:, at : at + step] = weight.astype(jnp.bfloat16)
        ones = jnp.ones((keys, 128), jnp.bfloat16)
        acc = jnp.dot(
            p_ref[...],
            jnp.concatenate([value, ones], axis=1),
            preferred_element_type=jnp.float32,
        )
        score = lax.dot_general(part, fresh_ref[0, :, lanes], NT, preferred_element_type=jnp.float32)
        weight = jnp.where(is_own, jnp.exp(score), 0.0).astype(jnp.bfloat16)
        acc = acc + jnp.dot(
            weight,
            jnp.concatenate([fresh_ref[1, :, lanes], ones[:patch]], axis=1),
            preferred_element_type=jnp.float32,
        )
        numer = jnp.where(low, acc[:rows, :128], acc[rows:, :128])
        out_ref[:, :, lanes] = numer.astype(jnp.bfloat16).reshape(count, patch, 128)
        for half in range(2):
            head = 2 * pair + half
            found = acc[half * rows : (half + 1) * rows, 128:]
            totals = jnp.where((lane == head) | (lane == 16 + head), found, totals)
    coarse = totals.astype(jnp.bfloat16)
    fine = (totals - coarse.astype(jnp.float32)).astype(jnp.bfloat16)
    out_ref[:, :, INNER:] = jnp.where(lane < 16, coarse, fine).reshape(count, patch, 128)


def attend(place, query, fresh, key_parts):
    rows, patch = query.shape[0], fresh.shape[1]
    keys = sum(p.shape[0] for p in key_parts) * patch
    return pl.pallas_call(
        attend_kernel,
        out_shape=jax.ShapeDtypeStruct((rows // patch, patch, INNER + 128), jnp.bfloat16),
        in_specs=[SMEM, VMEM, VMEM] + [HBM] * len(key_parts),
        out_specs=VMEM,
        scratch_shapes=[
            pltpu.VMEM((len(key_parts),) + key_parts[0].shape, jnp.bfloat16),
            pltpu.VMEM((2 * rows, keys), jnp.bfloat16),
            pltpu.SemaphoreType.DMA((len(key_parts),)),
        ],
        compiler_params=pltpu.CompilerParams(vmem_limit_bytes=56 * 1024 * 1024),
        cost_estimate=pl.CostEstimate(
            flops=rows * 4 * keys * INNER,
            bytes_accessed=4 * 1024 * 1024,
            transcendentals=rows * keys * HEADS,
        ),
    )(place, query, fresh, *key_parts)


def combine_kernel(parts_ref, out_ref):
    total = jnp.sum(parts_ref[:, :, INNER:].astype(jnp.float32), axis=0)
    low = lax.broadcasted_iota(jnp.int32, (1, 128), 1) < HEAD_DIM
    for pair in range(HEADS // 2):
        lanes = slice(pair * 128, pair * 128 + 128)
        numer = jnp.sum(parts_ref[:, :, lanes].astype(jnp.float32), axis=0)
        halves = [
            total[:, h : h + 1] + total[:, 16 + h : 17 + h] for h in (2 * pair, 2 * pair + 1)
        ]
        out_ref[:, lanes] = (numer / jnp.where(low, halves[0], halves[1])).astype(jnp.bfloat16)


def combine(parts):
    return pl.pallas_call(
        combine_kernel,
        out_shape=jax.ShapeDtypeStruct((parts.shape[1], INNER), jnp.bfloat16),
        in_specs=[VMEM],
        out_specs=VMEM,
    )(parts)


AXES = ("row", "col")
DEVICES = 256
NX, NY, NZ = 4, 4, 8
SHARE = 0b00100110
REST = 0b11111111 ^ SHARE


def place_of(x, y, z, core):
    return x * 64 + (y // 2) * 32 + z * 4 + (y % 2) * 2 + core


def moved(dx=0, dz=0, dcore=0):
    pairs = []
    for x in range(NX):
        for y in range(NY):
            for z in range(NZ):
                for core in range(2):
                    target = place_of((x + dx) % NX, y, (z + dz) % NZ, (core + dcore) % 2)
                    pairs.append((place_of(x, y, z, core), target))
    return sorted(pairs)


def groups_of(mask):
    found = {}
    for i in range(DEVICES):
        found.setdefault(i & ~mask, []).append(i)
    return list(found.values())


def exchange(value, mask):
    return lax.all_to_all(value, AXES, 0, 0, axis_index_groups=groups_of(mask))


def local(
    latent, gn_gain, gn_bias, w_in, b_in, ln_gain, ln_bias, w_query, w_key, w_value, stale_kv
):
    shared = 8
    with jax.named_scope("keys_z"):
        along_z = [lax.ppermute(stale_kv, AXES, moved(dz=d)) for d in (4, 2, 6)]
    with jax.named_scope("statistics"):
        here = statistics(latent, DEVICES)[:, None, :]
        stats = lax.all_to_all(here, AXES, 0, 0).reshape(DEVICES, 128)
    vectors = jnp.stack([gn_gain, gn_bias, b_in, ln_gain, ln_bias] + [jnp.zeros_like(b_in)] * 3)
    with jax.named_scope("keys_x"):
        line = jnp.stack([stale_kv] + along_z)
        parts = [line] + [lax.ppermute(line, AXES, moved(dx=d)) for d in (1, 3, 2)]
    stream, lnorm, query = project(stats, vectors, latent, w_in, w_query, shared)
    with jax.named_scope("queries"):
        query = exchange(query, SHARE).reshape(shared * latent.shape[0], INNER)
    fresh_kv = fresh_keys(lnorm, w_key, w_value)
    with jax.named_scope("keys_core"):
        parts = parts + [lax.ppermute(part, AXES, moved(dcore=1)) for part in parts]
    row, col = lax.axis_index("row"), lax.axis_index("col")
    place = ((row & 1) << 2) | (((col >> 2) & 1) << 1) | ((col >> 1) & 1)
    place = place.reshape(1).astype(jnp.int32)
    partial = attend(place, query, fresh_kv, parts)
    with jax.named_scope("partials"):
        attended = combine(exchange(partial, SHARE))
    return (stream, fresh_kv, attended)


def solution(mesh):
    placed = (
        P(AXES, None),
        P(),
        P(),
        P(),
        P(),
        P(),
        P(),
        P(),
        P(),
        P(),
        P(None, AXES, None),
    )
    return jax.shard_map(
        local,
        mesh=mesh,
        in_specs=placed,
        out_specs=(P(AXES, None), P(None, AXES, None), P(AXES, None)),
        check_vma=False,
    )
```

```python
import math
import jax
import jax.numpy as jnp
from jax import lax
from jax.experimental import pallas as pl
from jax.experimental.pallas import tpu as pltpu
from jax.sharding import PartitionSpec as P

GROUPS = 32
HEADS = 10
HEAD_DIM = 64
INNER = HEADS * HEAD_DIM
VMEM = pl.BlockSpec(memory_space=pltpu.VMEM)
SMEM = pl.BlockSpec(memory_space=pltpu.SMEM)
HBM = pl.BlockSpec(memory_space=pltpu.HBM)
NT = (((1,), (1,)), ((), ()))


def member_of(chans):
    width = chans // GROUPS
    first = lax.broadcasted_iota(jnp.int32, (chans, 128), 1) * width
    chan = lax.broadcasted_iota(jnp.int32, (chans, 128), 0)
    inside = (chan >= first) & (chan < first + width)
    return jnp.where(inside, 1.0, 0.0).astype(jnp.bfloat16)


def pieces(value):
    a = value.astype(jnp.bfloat16)
    rest = value - a.astype(jnp.float32)
    b = rest.astype(jnp.bfloat16)
    c = (rest - b.astype(jnp.float32)).astype(jnp.bfloat16)
    return jnp.concatenate([a, b, c], axis=0)


def to_groups(row, member):
    got = jnp.dot(pieces(row), member, preferred_element_type=jnp.float32)
    return got[0:1] + got[1:2] + got[2:3]


def to_channels(row, member):
    got = lax.dot_general(pieces(row), member, NT, preferred_element_type=jnp.float32)
    return got[0:1] + got[1:2] + got[2:3]


def statistics_kernel(x_ref, out_ref):
    rows, chans = x_ref.shape
    entries = rows * (chans // GROUPS)
    member = member_of(chans)
    x = x_ref[...].astype(jnp.float32)
    mean = to_groups(jnp.sum(x, axis=0, keepdims=True), member) * (1.0 / entries)
    off = x - to_channels(mean, member)
    square = to_groups(jnp.sum(off * off, axis=0, keepdims=True), member)
    lane = lax.broadcasted_iota(jnp.int32, (1, 128), 1)
    both = jnp.where(lane < GROUPS, mean, pltpu.roll(square, GROUPS, axis=1))
    out_ref[...] = jnp.broadcast_to(both, out_ref.shape)


def statistics(x, peers):
    return pl.pallas_call(
        statistics_kernel,
        out_shape=jax.ShapeDtypeStruct((peers, 128), jnp.float32),
        in_specs=[VMEM],
        out_specs=VMEM,
        compiler_params=pltpu.CompilerParams(vmem_limit_bytes=8 * 1024 * 1024),
    )(x)


def project_kernel(stats_ref, gain_ref, bias_ref, b_in_ref, ln_gain_ref, ln_bias_ref, x_ref, *refs):
    w_in_hbm, w_q_hbm, stream_ref, lnorm_ref, query_ref, w_in_ref, w_q_ref, sems = refs
    rows, chans = x_ref.shape
    parts = w_in_ref.shape[0] // 320
    copies = [
        pltpu.make_async_copy(
            w_in_hbm.at[pl.ds(i * 320, 320)], w_in_ref.at[pl.ds(i * 320, 320)], sems.at[i]
        )
        for i in range(parts)
    ] + [pltpu.make_async_copy(w_q_hbm, w_q_ref, sems.at[parts])]
    for copy in copies:
        copy.start()

    peers = stats_ref.shape[0]
    entries = rows * (chans // GROUPS)
    lane = lax.broadcasted_iota(jnp.int32, (1, 128), 1)
    stats = stats_ref[...]
    sums = jnp.sum(stats, axis=0, keepdims=True)
    mean = jnp.where(lane < GROUPS, sums * (1.0 / peers), 0.0)
    apart = jnp.where(lane < GROUPS, stats - mean, 0.0)
    square = pltpu.roll(sums, 128 - GROUPS, axis=1) + entries * jnp.sum(
        apart * apart, axis=0, keepdims=True
    )
    square = jnp.where(lane < GROUPS, square, 0.0)
    member = member_of(chans)
    scale = lax.rsqrt(square * (1.0 / (entries * peers)) + 1e-06)
    both = lax.dot_general(
        jnp.concatenate([pieces(mean), pieces(scale)], axis=0),
        member,
        NT,
        preferred_element_type=jnp.float32,
    )
    mean = both[0:1] + both[1:2] + both[2:3]
    scale = both[3:4] + both[4:5] + both[5:6]

    def row(ref):
        return ref[...].reshape(1, chans)

    x = x_ref[...].astype(jnp.float32)
    normed = ((x - mean) * scale * row(gain_ref) + row(bias_ref)).astype(jnp.bfloat16)
    stream = row(b_in_ref)
    for i in range(parts):
        copies[i].wait()
    stream = stream + jnp.dot(normed, w_in_ref[...], preferred_element_type=jnp.float32)
    stream = stream.astype(jnp.bfloat16)
    stream_ref[...] = stream
    wide = stream.astype(jnp.float32)
    token_mean = jnp.mean(wide, axis=-1, keepdims=True)
    token_dev = wide - token_mean
    token_var = jnp.mean(token_dev * token_dev, axis=-1, keepdims=True)
    lnorm = token_dev * lax.rsqrt(token_var + 1e-05) * row(ln_gain_ref) + row(ln_bias_ref)
    lnorm = lnorm.astype(jnp.bfloat16)
    lnorm_ref[...] = lnorm
    copies[parts].wait()
    query = jnp.dot(lnorm, w_q_ref[...], preferred_element_type=jnp.float32)
    query = query.astype(jnp.bfloat16) * jnp.bfloat16(1.0 / math.sqrt(HEAD_DIM))
    query_ref[...] = jnp.broadcast_to(query[None], query_ref.shape)


def project(stats, vectors, x, w_in, w_query, copies):
    patch, chans = x.shape
    bf16 = jnp.bfloat16
    return pl.pallas_call(
        project_kernel,
        out_shape=(
            jax.ShapeDtypeStruct((patch, chans), bf16),
            jax.ShapeDtypeStruct((patch, chans), bf16),
            jax.ShapeDtypeStruct((copies, patch, INNER), bf16),
        ),
        in_specs=[VMEM] * 7 + [HBM] * 2,
        out_specs=(VMEM, VMEM, VMEM),
        scratch_shapes=[
            pltpu.VMEM(w_in.shape, bf16),
            pltpu.VMEM(w_query.shape, bf16),
            pltpu.SemaphoreType.DMA((5,)),
        ],
        compiler_params=pltpu.CompilerParams(vmem_limit_bytes=56 * 1024 * 1024),
        cost_estimate=pl.CostEstimate(
            flops=patch * 2 * chans * (chans + INNER),
            bytes_accessed=6 * 1024 * 1024,
            transcendentals=patch,
        ),
    )(stats, *vectors, x, w_in, w_query)


def fresh_kernel(x_ref, w_k_hbm, w_v_hbm, out_ref, w_ref, sems):
    copies = [
        pltpu.make_async_copy(source, w_ref.at[i], sems.at[i])
        for i, source in enumerate((w_k_hbm, w_v_hbm))
    ]
    for copy in copies:
        copy.start()
    for i, copy in enumerate(copies):
        copy.wait()
        out_ref[i] = jnp.dot(x_ref[...], w_ref[i], preferred_element_type=jnp.float32).astype(
            jnp.bfloat16
        )


def fresh_keys(x, w_key, w_value):
    return pl.pallas_call(
        fresh_kernel,
        out_shape=jax.ShapeDtypeStruct((2, x.shape[0], INNER), jnp.bfloat16),
        in_specs=[VMEM, HBM, HBM],
        out_specs=VMEM,
        scratch_shapes=[
            pltpu.VMEM((2,) + w_key.shape, jnp.bfloat16),
            pltpu.SemaphoreType.DMA((2,)),
        ],
        compiler_params=pltpu.CompilerParams(vmem_limit_bytes=56 * 1024 * 1024),
    )(x, w_key, w_value)


def attend_kernel(place_ref, q_hbm, fresh_ref, *refs):
    sources, refs = refs[:-9], refs[-9:]
    out_ref, kv_ref, p_ref, q_ref, more_ref, numer_ref, total_ref, sems, q_sem = refs
    q_copy = pltpu.make_async_copy(q_hbm, q_ref, q_sem)
    q_copy.start()
    copies = [
        pltpu.make_async_copy(source, kv_ref.at[i], sems.at[i])
        for i, source in enumerate(sources)
    ]
    for copy in copies:
        copy.start()
    patch = fresh_ref.shape[1]
    rows = q_ref.shape[0]
    count = rows // patch
    place = place_ref[0]
    own = place * patch
    lane = lax.broadcasted_iota(jnp.int32, (1, 128), 1)
    low = lane < HEAD_DIM
    pairs = [slice(at * 128, at * 128 + 128) for at in range(HEADS // 2)]

    def two_heads(part):
        zero = jnp.zeros_like(part)
        return jnp.concatenate([jnp.where(low, part, zero), jnp.where(low, zero, part)], axis=0)

    def with_ones(value):
        return jnp.concatenate([value, jnp.ones((value.shape[0], 128), jnp.bfloat16)], axis=1)

    q_copy.wait()
    for pair, lanes in enumerate(pairs):
        score = lax.dot_general(
            two_heads(q_ref[pl.ds(own, patch), lanes]),
            fresh_ref[0, :, lanes],
            NT,
            preferred_element_type=jnp.float32,
        )
        more_ref[pair] = jnp.dot(
            jnp.exp(score).astype(jnp.bfloat16),
            with_ones(fresh_ref[1, :, lanes]),
            preferred_element_type=jnp.float32,
        )
    for copy in copies:
        copy.wait()

    keys = p_ref.shape[1]
    row = lax.broadcasted_iota(jnp.int32, (2 * rows, 1), 0)
    row = jnp.where(row >= rows, row - rows, row)
    is_own = (row >= own) & (row < own + patch)
    totals = jnp.zeros((rows, 128), jnp.float32)
    own_totals = jnp.zeros((patch, 128), jnp.float32)
    step = 128
    for pair, lanes in enumerate(pairs):
        query = two_heads(q_ref[:, lanes])
        key = kv_ref[:, :, 0, :, lanes].reshape(keys, 128)
        value = kv_ref[:, :, 1, :, lanes].reshape(keys, 128)
        for at in range(0, keys, step):
            score = lax.dot_general(
                query, key[at : at + step], NT, preferred_element_type=jnp.float32
            )
            weight = jnp.exp(score)
            if at == 0:
                column = lax.broadcasted_iota(jnp.int32, (1, step), 1)
                weight = jnp.where(is_own & (column < patch), 0.0, weight)
            p_ref[:, at : at + step] = weight.astype(jnp.bfloat16)
        acc = jnp.dot(p_ref[...], with_ones(value), preferred_element_type=jnp.float32)
        numer = jnp.where(low, acc[:rows, :128], acc[rows:, :128])
        out_ref[:, :, lanes] = numer.astype(jnp.bfloat16).reshape(count, patch, 128)
        numer_ref[...] = numer
        more = more_ref[pair]
        mine = numer_ref[pl.ds(own, patch), :] + jnp.where(
            low, more[:patch, :128], more[patch:, :128]
        )
        out_ref[place, :, lanes] = mine.astype(jnp.bfloat16)
        for half in range(2):
            head = 2 * pair + half
            here = (lane == head) | (lane == 16 + head)
            totals = jnp.where(here, acc[half * rows : (half + 1) * rows, 128:], totals)
            own_totals = jnp.where(here, more[half * patch : (half + 1) * patch, 128:], own_totals)

    def coded(total):
        coarse = total.astype(jnp.bfloat16)
        fine = (total - coarse.astype(jnp.float32)).astype(jnp.bfloat16)
        return jnp.where(lane < 16, coarse, fine)

    out_ref[:, :, INNER:] = coded(totals).reshape(count, patch, 128)
    total_ref[...] = totals
    out_ref[place, :, INNER:] = coded(total_ref[pl.ds(own, patch), :] + own_totals)


def attend(place, query, fresh, key_parts):
    rows, patch = query.shape[0], fresh.shape[1]
    keys = sum(p.shape[0] for p in key_parts) * patch
    return pl.pallas_call(
        attend_kernel,
        out_shape=jax.ShapeDtypeStruct((rows // patch, patch, INNER + 128), jnp.bfloat16),
        in_specs=[SMEM, HBM, VMEM] + [HBM] * len(key_parts),
        out_specs=VMEM,
        scratch_shapes=[
            pltpu.VMEM((len(key_parts),) + key_parts[0].shape, jnp.bfloat16),
            pltpu.VMEM((2 * rows, keys), jnp.bfloat16),
            pltpu.VMEM(query.shape, jnp.bfloat16),
            pltpu.VMEM((HEADS // 2, 2 * patch, 256), jnp.float32),
            pltpu.VMEM((rows, 128), jnp.float32),
            pltpu.VMEM((rows, 128), jnp.float32),
            pltpu.SemaphoreType.DMA((len(key_parts),)),
            pltpu.SemaphoreType.DMA(()),
        ],
        compiler_params=pltpu.CompilerParams(vmem_limit_bytes=56 * 1024 * 1024),
        cost_estimate=pl.CostEstimate(
            flops=rows * 4 * keys * INNER,
            bytes_accessed=4 * 1024 * 1024,
            transcendentals=rows * keys * HEADS,
        ),
    )(place, query, fresh, *key_parts)


def combine_kernel(parts_ref, out_ref):
    total = jnp.sum(parts_ref[:, :, INNER:].astype(jnp.float32), axis=0)
    low = lax.broadcasted_iota(jnp.int32, (1, 128), 1) < HEAD_DIM
    for pair in range(HEADS // 2):
        lanes = slice(pair * 128, pair * 128 + 128)
        numer = jnp.sum(parts_ref[:, :, lanes].astype(jnp.float32), axis=0)
        halves = [
            total[:, h : h + 1] + total[:, 16 + h : 17 + h] for h in (2 * pair, 2 * pair + 1)
        ]
        out_ref[:, lanes] = (numer / jnp.where(low, halves[0], halves[1])).astype(jnp.bfloat16)


def combine(parts):
    return pl.pallas_call(
        combine_kernel,
        out_shape=jax.ShapeDtypeStruct((parts.shape[1], INNER), jnp.bfloat16),
        in_specs=[VMEM],
        out_specs=VMEM,
        compiler_params=pltpu.CompilerParams(vmem_limit_bytes=8 * 1024 * 1024),
    )(parts)


AXES = ("row", "col")
DEVICES = 256
NX, NY, NZ = 4, 4, 8
SHARE = 0b00100110
REST = 0b11111111 ^ SHARE


def place_of(x, y, z, core):
    return x * 64 + (y // 2) * 32 + z * 4 + (y % 2) * 2 + core


def moved(dx=0, dz=0, dcore=0):
    pairs = []
    for x in range(NX):
        for y in range(NY):
            for z in range(NZ):
                for core in range(2):
                    target = place_of((x + dx) % NX, y, (z + dz) % NZ, (core + dcore) % 2)
                    pairs.append((place_of(x, y, z, core), target))
    return sorted(pairs)


def groups_of(mask):
    found = {}
    for i in range(DEVICES):
        found.setdefault(i & ~mask, []).append(i)
    return list(found.values())


def exchange(value, mask):
    return lax.all_to_all(value, AXES, 0, 0, axis_index_groups=groups_of(mask))


def local(
    latent, gn_gain, gn_bias, w_in, b_in, ln_gain, ln_bias, w_query, w_key, w_value, stale_kv
):
    shared = 8
    with jax.named_scope("keys_z"):
        along_z = [lax.ppermute(stale_kv, AXES, moved(dz=d)) for d in (4, 2, 6)]
    with jax.named_scope("statistics"):
        here = statistics(latent, DEVICES)[:, None, :]
        stats = lax.all_to_all(here, AXES, 0, 0).reshape(DEVICES, 128)
    vectors = [gn_gain, gn_bias, b_in, ln_gain, ln_bias]
    with jax.named_scope("keys_x"):
        line = jnp.stack([stale_kv] + along_z)
        parts = [line] + [lax.ppermute(line, AXES, moved(dx=d)) for d in (1, 3, 2)]
    stream, lnorm, query = project(stats, vectors, latent, w_in, w_query, shared)
    with jax.named_scope("queries"):
        query = exchange(query, SHARE).reshape(shared * latent.shape[0], INNER)
    fresh_kv = fresh_keys(lnorm, w_key, w_value)
    with jax.named_scope("keys_core"):
        parts = parts + [lax.ppermute(part, AXES, moved(dcore=1)) for part in parts]
    row, col = lax.axis_index("row"), lax.axis_index("col")
    place = ((row & 1) << 2) | (((col >> 2) & 1) << 1) | ((col >> 1) & 1)
    place = place.reshape(1).astype(jnp.int32)
    partial = attend(place, query, fresh_kv, parts)
    with jax.named_scope("partials"):
        attended = combine(exchange(partial, SHARE))
    return (stream, fresh_kv, attended)


def solution(mesh):
    placed = (
        P(AXES, None),
        P(),
        P(),
        P(),
        P(),
        P(),
        P(),
        P(),
        P(),
        P(),
        P(None, AXES, None),
    )
    return jax.shard_map(
        local,
        mesh=mesh,
        in_specs=placed,
        out_specs=(P(AXES, None), P(None, AXES, None), P(AXES, None)),
        check_vma=False,
    )
```

```python
import functools
import math
import jax
import jax.numpy as jnp
from jax import lax
from jax.experimental import pallas as pl
from jax.experimental.pallas import tpu as pltpu
from jax.sharding import PartitionSpec as P

GROUPS = 32
HEADS = 10
HEAD_DIM = 64
INNER = HEADS * HEAD_DIM
VMEM = pl.BlockSpec(memory_space=pltpu.VMEM)
SMEM = pl.BlockSpec(memory_space=pltpu.SMEM)
HBM = pl.BlockSpec(memory_space=pltpu.HBM)
NT = (((1,), (1,)), ((), ()))
ATT_LIMIT = 16 * 1024 * 1024


def member_of(chans):
    width = chans // GROUPS
    first = lax.broadcasted_iota(jnp.int32, (chans, 128), 1) * width
    chan = lax.broadcasted_iota(jnp.int32, (chans, 128), 0)
    inside = (chan >= first) & (chan < first + width)
    return jnp.where(inside, 1.0, 0.0).astype(jnp.bfloat16)


def pieces(value):
    a = value.astype(jnp.bfloat16)
    rest = value - a.astype(jnp.float32)
    b = rest.astype(jnp.bfloat16)
    c = (rest - b.astype(jnp.float32)).astype(jnp.bfloat16)
    return jnp.concatenate([a, b, c], axis=0)


def to_groups(row, member):
    got = jnp.dot(pieces(row), member, preferred_element_type=jnp.float32)
    return got[0:1] + got[1:2] + got[2:3]


def to_channels(row, member):
    got = lax.dot_general(pieces(row), member, NT, preferred_element_type=jnp.float32)
    return got[0:1] + got[1:2] + got[2:3]


def statistics_kernel(x_ref, out_ref):
    rows, chans = x_ref.shape
    entries = rows * (chans // GROUPS)
    member = member_of(chans)
    x = x_ref[...].astype(jnp.float32)
    mean = to_groups(jnp.sum(x, axis=0, keepdims=True), member) * (1.0 / entries)
    off = x - to_channels(mean, member)
    square = to_groups(jnp.sum(off * off, axis=0, keepdims=True), member)
    lane = lax.broadcasted_iota(jnp.int32, (1, 128), 1)
    both = jnp.where(lane < GROUPS, mean, pltpu.roll(square, GROUPS, axis=1))
    out_ref[...] = jnp.broadcast_to(both[:, : 2 * GROUPS], out_ref.shape)


def statistics(x, peers):
    return pl.pallas_call(
        statistics_kernel,
        out_shape=jax.ShapeDtypeStruct((peers, 2 * GROUPS), jnp.float32),
        in_specs=[VMEM],
        out_specs=VMEM,
        compiler_params=pltpu.CompilerParams(vmem_limit_bytes=8 * 1024 * 1024),
    )(x)


def coefficients_kernel(entries, stats_ref, out_ref):
    peers = stats_ref.shape[0]
    means = stats_ref[:, :GROUPS]
    mean = jnp.sum(means, axis=0, keepdims=True) * (1.0 / peers)
    apart = means - mean
    square = jnp.sum(stats_ref[:, GROUPS:] + entries * (apart * apart), axis=0, keepdims=True)
    scale = lax.rsqrt(square * (1.0 / (entries * peers)) + 1e-06)
    rest = jnp.zeros((1, 128 - GROUPS), jnp.float32)
    mean = jnp.concatenate([mean, rest], axis=1)
    scale = jnp.concatenate([scale, rest], axis=1)
    both = lax.dot_general(
        jnp.concatenate([pieces(mean), pieces(scale)], axis=0),
        member_of(out_ref.shape[1]),
        NT,
        preferred_element_type=jnp.float32,
    )
    out_ref[...] = jnp.concatenate(
        [both[at : at + 1] + both[at + 1 : at + 2] + both[at + 2 : at + 3] for at in (0, 3)], axis=0
    )


def coefficients(stats, entries, chans):
    return pl.pallas_call(
        functools.partial(coefficients_kernel, entries),
        out_shape=jax.ShapeDtypeStruct((2, chans), jnp.float32),
        in_specs=[VMEM],
        out_specs=VMEM,
        compiler_params=pltpu.CompilerParams(vmem_limit_bytes=8 * 1024 * 1024),
    )(stats)


def attend_kernel(place_ref, q_ref, x_ref, w_k_hbm, w_v_hbm, *refs):
    sources, refs = refs[:-9], refs[-9:]
    out_ref, fresh_ref, w_ref, kv_ref, p_ref, more_ref, numer_ref, total_ref, sems = refs
    copies = [
        pltpu.make_async_copy(source, target, sems.at[i])
        for i, (source, target) in enumerate(
            [(w_k_hbm, w_ref.at[0]), (w_v_hbm, w_ref.at[1])]
            + [(source, kv_ref.at[i]) for i, source in enumerate(sources)]
        )
    ]
    for copy in copies:
        copy.start()
    patch = x_ref.shape[0]
    rows = q_ref.shape[0]
    count = rows // patch
    place = place_ref[0]
    own = place * patch
    lane = lax.broadcasted_iota(jnp.int32, (1, 128), 1)
    low = lane < HEAD_DIM
    pairs = [slice(at * 128, at * 128 + 128) for at in range(HEADS // 2)]

    def two_heads(part):
        zero = jnp.zeros_like(part)
        return jnp.concatenate([jnp.where(low, part, zero), jnp.where(low, zero, part)], axis=0)

    def with_ones(value):
        return jnp.concatenate([value, jnp.ones((value.shape[0], 128), jnp.bfloat16)], axis=1)

    for i in range(2):
        copies[i].wait()
        fresh_ref[i] = jnp.dot(x_ref[...], w_ref[i], preferred_element_type=jnp.float32).astype(
            jnp.bfloat16
        )
    for pair, lanes in enumerate(pairs):
        score = lax.dot_general(
            two_heads(q_ref[pl.ds(own, patch), lanes]),
            fresh_ref[0, :, lanes],
            NT,
            preferred_element_type=jnp.float32,
        )
        more_ref[pair] = jnp.dot(
            jnp.exp(score).astype(jnp.bfloat16),
            with_ones(fresh_ref[1, :, lanes]),
            preferred_element_type=jnp.float32,
        )
    for copy in copies[2:]:
        copy.wait()

    keys = p_ref.shape[1]
    row = lax.broadcasted_iota(jnp.int32, (2 * rows, 1), 0)
    row = jnp.where(row >= rows, row - rows, row)
    is_own = (row >= own) & (row < own + patch)
    totals = jnp.zeros((rows, 128), jnp.float32)
    own_totals = jnp.zeros((patch, 128), jnp.float32)
    step = 128
    for pair, lanes in enumerate(pairs):
        query = two_heads(q_ref[:, lanes])
        key = kv_ref[:, :, 0, :, lanes].reshape(keys, 128)
        value = kv_ref[:, :, 1, :, lanes].reshape(keys, 128)
        for at in range(0, keys, step):
            score = lax.dot_general(
                query, key[at : at + step], NT, preferred_element_type=jnp.float32
            )
            weight = jnp.exp(score)
            if at == 0:
                column = lax.broadcasted_iota(jnp.int32, (1, step), 1)
                weight = jnp.where(is_own & (column < patch), 0.0, weight)
            p_ref[:, at : at + step] = weight.astype(jnp.bfloat16)
        acc = jnp.dot(p_ref[...], with_ones(value), preferred_element_type=jnp.float32)
        numer = jnp.where(low, acc[:rows, :128], acc[rows:, :128])
        out_ref[:, :, lanes] = numer.astype(jnp.bfloat16).reshape(count, patch, 128)
        numer_ref[...] = numer
        more = more_ref[pair]
        mine = numer_ref[pl.ds(own, patch), :] + jnp.where(
            low, more[:patch, :128], more[patch:, :128]
        )
        out_ref[place, :, lanes] = mine.astype(jnp.bfloat16)
        for half in range(2):
            head = 2 * pair + half
            here = (lane == head) | (lane == 16 + head)
            totals = jnp.where(here, acc[half * rows : (half + 1) * rows, 128:], totals)
            own_totals = jnp.where(here, more[half * patch : (half + 1) * patch, 128:], own_totals)

    def coded(total):
        coarse = total.astype(jnp.bfloat16)
        fine = (total - coarse.astype(jnp.float32)).astype(jnp.bfloat16)
        return jnp.where(lane < 16, coarse, fine)

    out_ref[:, :, INNER:] = coded(totals).reshape(count, patch, 128)
    total_ref[...] = totals
    out_ref[place, :, INNER:] = coded(total_ref[pl.ds(own, patch), :] + own_totals)


def attend(place, query, x, w_key, w_value, key_parts):
    rows, patch = query.shape[0], x.shape[0]
    keys = sum(p.shape[0] for p in key_parts) * patch
    return pl.pallas_call(
        attend_kernel,
        out_shape=(
            jax.ShapeDtypeStruct((rows // patch, patch, INNER + 128), jnp.bfloat16),
            jax.ShapeDtypeStruct((2, patch, INNER), jnp.bfloat16),
        ),
        in_specs=[SMEM, VMEM, VMEM] + [HBM] * (2 + len(key_parts)),
        out_specs=(VMEM, VMEM),
        scratch_shapes=[
            pltpu.VMEM((2,) + w_key.shape, jnp.bfloat16),
            pltpu.VMEM((len(key_parts),) + key_parts[0].shape, jnp.bfloat16),
            pltpu.VMEM((2 * rows, keys), jnp.bfloat16),
            pltpu.VMEM((HEADS // 2, 2 * patch, 256), jnp.float32),
            pltpu.VMEM((rows, 128), jnp.float32),
            pltpu.VMEM((rows, 128), jnp.float32),
            pltpu.SemaphoreType.DMA((2 + len(key_parts),)),
        ],
        compiler_params=pltpu.CompilerParams(vmem_limit_bytes=ATT_LIMIT),
        cost_estimate=pl.CostEstimate(
            flops=rows * 4 * keys * INNER,
            bytes_accessed=8 * 1024 * 1024,
            transcendentals=rows * keys * HEADS,
        ),
    )(place, query, x, w_key, w_value, *key_parts)


def combine_kernel(parts_ref, out_ref):
    total = jnp.sum(parts_ref[:, :, INNER:].astype(jnp.float32), axis=0)
    low = lax.broadcasted_iota(jnp.int32, (1, 128), 1) < HEAD_DIM
    for pair in range(HEADS // 2):
        lanes = slice(pair * 128, pair * 128 + 128)
        numer = jnp.sum(parts_ref[:, :, lanes].astype(jnp.float32), axis=0)
        halves = [
            total[:, h : h + 1] + total[:, 16 + h : 17 + h] for h in (2 * pair, 2 * pair + 1)
        ]
        out_ref[:, lanes] = (numer / jnp.where(low, halves[0], halves[1])).astype(jnp.bfloat16)


def combine(parts):
    return pl.pallas_call(
        combine_kernel,
        out_shape=jax.ShapeDtypeStruct((parts.shape[1], INNER), jnp.bfloat16),
        in_specs=[VMEM],
        out_specs=VMEM,
        compiler_params=pltpu.CompilerParams(vmem_limit_bytes=8 * 1024 * 1024),
    )(parts)


AXES = ("row", "col")
DEVICES = 256
NX, NY, NZ = 4, 4, 8
SHARE = 0b00100110
REST = 0b11111111 ^ SHARE


def place_of(x, y, z, core):
    return x * 64 + (y // 2) * 32 + z * 4 + (y % 2) * 2 + core


def moved(dx=0, dz=0, dcore=0):
    pairs = []
    for x in range(NX):
        for y in range(NY):
            for z in range(NZ):
                for core in range(2):
                    target = place_of((x + dx) % NX, y, (z + dz) % NZ, (core + dcore) % 2)
                    pairs.append((place_of(x, y, z, core), target))
    return sorted(pairs)


def groups_of(mask):
    found = {}
    for i in range(DEVICES):
        found.setdefault(i & ~mask, []).append(i)
    return list(found.values())


def exchange(value, mask):
    return lax.all_to_all(value, AXES, 0, 0, axis_index_groups=groups_of(mask))


def local(
    latent, gn_gain, gn_bias, w_in, b_in, ln_gain, ln_bias, w_query, w_key, w_value, stale_kv
):
    shared = 8
    with jax.named_scope("keys_z"):
        along_z = [lax.ppermute(stale_kv, AXES, moved(dz=d)) for d in (4, 2, 6)]
    with jax.named_scope("statistics"):
        here = statistics(latent, DEVICES)[:, None, :]
        stats = lax.all_to_all(here, AXES, 0, 0).reshape(DEVICES, 2 * GROUPS)
    with jax.named_scope("keys_x"):
        line = jnp.stack([stale_kv] + along_z)
        parts = [line] + [lax.ppermute(line, AXES, moved(dx=d)) for d in (1, 3, 2)]
    rows, chans = latent.shape
    group = coefficients(stats, rows * (chans // GROUPS), chans)
    scaled = (latent.astype(jnp.float32) - group[0:1]) * group[1:2]
    normed = (scaled * gn_gain + gn_bias).astype(jnp.bfloat16)
    stream = (jnp.dot(normed, w_in, preferred_element_type=jnp.float32) + b_in).astype(jnp.bfloat16)
    wide = stream.astype(jnp.float32)
    token_mean = jnp.mean(wide, axis=-1, keepdims=True)
    token_dev = wide - token_mean
    token_var = jnp.mean(token_dev * token_dev, axis=-1, keepdims=True)
    lnorm = (token_dev * lax.rsqrt(token_var + 1e-05) * ln_gain + ln_bias).astype(jnp.bfloat16)
    query = jnp.dot(lnorm, w_query, preferred_element_type=jnp.float32).astype(jnp.bfloat16)
    query = query * jnp.bfloat16(1.0 / math.sqrt(HEAD_DIM))
    query = jnp.broadcast_to(query[None], (shared, rows, INNER))
    with jax.named_scope("queries"):
        query = exchange(query, SHARE).reshape(shared * latent.shape[0], INNER)
    with jax.named_scope("keys_core"):
        parts = parts + [lax.ppermute(part, AXES, moved(dcore=1)) for part in parts]
    row, col = lax.axis_index("row"), lax.axis_index("col")
    place = ((row & 1) << 2) | (((col >> 2) & 1) << 1) | ((col >> 1) & 1)
    place = place.reshape(1).astype(jnp.int32)
    partial, fresh_kv = attend(place, query, lnorm, w_key, w_value, parts)
    with jax.named_scope("partials"):
        attended = combine(exchange(partial, SHARE))
    return (stream, fresh_kv, attended)


def solution(mesh):
    placed = (
        P(AXES, None),
        P(),
        P(),
        P(),
        P(),
        P(),
        P(),
        P(),
        P(),
        P(),
        P(None, AXES, None),
    )
    return jax.shard_map(
        local,
        mesh=mesh,
        in_specs=placed,
        out_specs=(P(AXES, None), P(None, AXES, None), P(AXES, None)),
        check_vma=False,
    )
```

```python
import functools
import math
import jax
import jax.numpy as jnp
from jax import lax
from jax.experimental import pallas as pl
from jax.experimental.pallas import tpu as pltpu
from jax.sharding import PartitionSpec as P

GROUPS = 32
HEADS = 10
HEAD_DIM = 64
INNER = HEADS * HEAD_DIM
VMEM = pl.BlockSpec(memory_space=pltpu.VMEM)
SMEM = pl.BlockSpec(memory_space=pltpu.SMEM)
HBM = pl.BlockSpec(memory_space=pltpu.HBM)
NT = (((1,), (1,)), ((), ()))
ATT_LIMIT = 16 * 1024 * 1024


def member_of(chans):
    width = chans // GROUPS
    first = lax.broadcasted_iota(jnp.int32, (chans, 128), 1) * width
    chan = lax.broadcasted_iota(jnp.int32, (chans, 128), 0)
    inside = (chan >= first) & (chan < first + width)
    return jnp.where(inside, 1.0, 0.0).astype(jnp.bfloat16)


def pieces(value):
    a = value.astype(jnp.bfloat16)
    rest = value - a.astype(jnp.float32)
    b = rest.astype(jnp.bfloat16)
    c = (rest - b.astype(jnp.float32)).astype(jnp.bfloat16)
    return jnp.concatenate([a, b, c], axis=0)


def to_groups(row, member):
    got = jnp.dot(pieces(row), member, preferred_element_type=jnp.float32)
    return got[0:1] + got[1:2] + got[2:3]


def to_channels(row, member):
    got = lax.dot_general(pieces(row), member, NT, preferred_element_type=jnp.float32)
    return got[0:1] + got[1:2] + got[2:3]


def statistics_kernel(x_ref, out_ref):
    rows, chans = x_ref.shape
    entries = rows * (chans // GROUPS)
    member = member_of(chans)
    x = x_ref[...].astype(jnp.float32)
    mean = to_groups(jnp.sum(x, axis=0, keepdims=True), member) * (1.0 / entries)
    off = x - to_channels(mean, member)
    square = to_groups(jnp.sum(off * off, axis=0, keepdims=True), member)
    lane = lax.broadcasted_iota(jnp.int32, (1, 128), 1)
    both = jnp.where(lane < GROUPS, mean, pltpu.roll(square, GROUPS, axis=1))
    out_ref[...] = jnp.broadcast_to(both[:, : 2 * GROUPS], out_ref.shape)


def statistics(x, peers):
    return pl.pallas_call(
        statistics_kernel,
        out_shape=jax.ShapeDtypeStruct((peers, 2 * GROUPS), jnp.float32),
        in_specs=[VMEM],
        out_specs=VMEM,
        compiler_params=pltpu.CompilerParams(vmem_limit_bytes=8 * 1024 * 1024),
    )(x)


def coefficients_kernel(entries, stats_ref, out_ref):
    peers = stats_ref.shape[0]
    means = stats_ref[:, :GROUPS]
    mean = jnp.sum(means, axis=0, keepdims=True) * (1.0 / peers)
    apart = means - mean
    square = jnp.sum(stats_ref[:, GROUPS:] + entries * (apart * apart), axis=0, keepdims=True)
    scale = lax.rsqrt(square * (1.0 / (entries * peers)) + 1e-06)
    rest = jnp.zeros((1, 128 - GROUPS), jnp.float32)
    mean = jnp.concatenate([mean, rest], axis=1)
    scale = jnp.concatenate([scale, rest], axis=1)
    both = lax.dot_general(
        jnp.concatenate([pieces(mean), pieces(scale)], axis=0),
        member_of(out_ref.shape[1]),
        NT,
        preferred_element_type=jnp.float32,
    )
    out_ref[...] = jnp.concatenate(
        [both[at : at + 1] + both[at + 1 : at + 2] + both[at + 2 : at + 3] for at in (0, 3)], axis=0
    )


def coefficients(stats, entries, chans):
    return pl.pallas_call(
        functools.partial(coefficients_kernel, entries),
        out_shape=jax.ShapeDtypeStruct((2, chans), jnp.float32),
        in_specs=[VMEM],
        out_specs=VMEM,
        compiler_params=pltpu.CompilerParams(vmem_limit_bytes=8 * 1024 * 1024),
    )(stats)


def attend_kernel(place_ref, q_ref, fresh_ref, *refs):
    sources, refs = refs[:-7], refs[-7:]
    out_ref, kv_ref, p_ref, more_ref, numer_ref, total_ref, sems = refs
    copies = [
        pltpu.make_async_copy(source, kv_ref.at[i], sems.at[i])
        for i, source in enumerate(sources)
    ]
    for copy in copies:
        copy.start()
    patch = fresh_ref.shape[1]
    rows = q_ref.shape[0]
    count = rows // patch
    place = place_ref[0]
    own = place * patch
    lane = lax.broadcasted_iota(jnp.int32, (1, 128), 1)
    low = lane < HEAD_DIM
    pairs = [slice(at * 128, at * 128 + 128) for at in range(HEADS // 2)]

    def two_heads(part):
        zero = jnp.zeros_like(part)
        return jnp.concatenate([jnp.where(low, part, zero), jnp.where(low, zero, part)], axis=0)

    def with_ones(value):
        return jnp.concatenate([value, jnp.ones((value.shape[0], 128), jnp.bfloat16)], axis=1)

    for pair, lanes in enumerate(pairs):
        score = lax.dot_general(
            two_heads(q_ref[pl.ds(own, patch), lanes]),
            fresh_ref[0, :, lanes],
            NT,
            preferred_element_type=jnp.float32,
        )
        more_ref[pair] = jnp.dot(
            jnp.exp(score).astype(jnp.bfloat16),
            with_ones(fresh_ref[1, :, lanes]),
            preferred_element_type=jnp.float32,
        )
    for copy in copies:
        copy.wait()

    keys = p_ref.shape[1]
    row = lax.broadcasted_iota(jnp.int32, (2 * rows, 1), 0)
    row = jnp.where(row >= rows, row - rows, row)
    is_own = (row >= own) & (row < own + patch)
    totals = jnp.zeros((rows, 128), jnp.float32)
    own_totals = jnp.zeros((patch, 128), jnp.float32)
    step = 128
    for pair, lanes in enumerate(pairs):
        query = two_heads(q_ref[:, lanes])
        key = kv_ref[:, :, 0, :, lanes].reshape(keys, 128)
        value = kv_ref[:, :, 1, :, lanes].reshape(keys, 128)
        for at in range(0, keys, step):
            score = lax.dot_general(
                query, key[at : at + step], NT, preferred_element_type=jnp.float32
            )
            weight = jnp.exp(score)
            if at == 0:
                column = lax.broadcasted_iota(jnp.int32, (1, step), 1)
                weight = jnp.where(is_own & (column < patch), 0.0, weight)
            p_ref[:, at : at + step] = weight.astype(jnp.bfloat16)
        acc = jnp.dot(p_ref[...], with_ones(value), preferred_element_type=jnp.float32)
        numer = jnp.where(low, acc[:rows, :128], acc[rows:, :128])
        out_ref[:, :, lanes] = numer.astype(jnp.bfloat16).reshape(count, patch, 128)
        numer_ref[...] = numer
        more = more_ref[pair]
        mine = numer_ref[pl.ds(own, patch), :] + jnp.where(
            low, more[:patch, :128], more[patch:, :128]
        )
        out_ref[place, :, lanes] = mine.astype(jnp.bfloat16)
        for half in range(2):
            head = 2 * pair + half
            here = (lane == head) | (lane == 16 + head)
            totals = jnp.where(here, acc[half * rows : (half + 1) * rows, 128:], totals)
            own_totals = jnp.where(here, more[half * patch : (half + 1) * patch, 128:], own_totals)

    def coded(total):
        coarse = total.astype(jnp.bfloat16)
        fine = (total - coarse.astype(jnp.float32)).astype(jnp.bfloat16)
        return jnp.where(lane < 16, coarse, fine)

    out_ref[:, :, INNER:] = coded(totals).reshape(count, patch, 128)
    total_ref[...] = totals
    out_ref[place, :, INNER:] = coded(total_ref[pl.ds(own, patch), :] + own_totals)


def attend(place, query, fresh, key_parts):
    rows, patch = query.shape[0], fresh.shape[1]
    keys = sum(p.shape[0] for p in key_parts) * patch
    return pl.pallas_call(
        attend_kernel,
        out_shape=jax.ShapeDtypeStruct((rows // patch, patch, INNER + 128), jnp.bfloat16),
        in_specs=[SMEM, VMEM, VMEM] + [HBM] * len(key_parts),
        out_specs=VMEM,
        scratch_shapes=[
            pltpu.VMEM((len(key_parts),) + key_parts[0].shape, jnp.bfloat16),
            pltpu.VMEM((2 * rows, keys), jnp.bfloat16),
            pltpu.VMEM((HEADS // 2, 2 * patch, 256), jnp.float32),
            pltpu.VMEM((rows, 128), jnp.float32),
            pltpu.VMEM((rows, 128), jnp.float32),
            pltpu.SemaphoreType.DMA((len(key_parts),)),
        ],
        compiler_params=pltpu.CompilerParams(vmem_limit_bytes=ATT_LIMIT),
        cost_estimate=pl.CostEstimate(
            flops=rows * 4 * keys * INNER,
            bytes_accessed=4 * 1024 * 1024,
            transcendentals=rows * keys * HEADS,
        ),
    )(place, query, fresh, *key_parts)


def combine_kernel(parts_ref, out_ref):
    total = jnp.sum(parts_ref[:, :, INNER:].astype(jnp.float32), axis=0)
    low = lax.broadcasted_iota(jnp.int32, (1, 128), 1) < HEAD_DIM
    for pair in range(HEADS // 2):
        lanes = slice(pair * 128, pair * 128 + 128)
        numer = jnp.sum(parts_ref[:, :, lanes].astype(jnp.float32), axis=0)
        halves = [
            total[:, h : h + 1] + total[:, 16 + h : 17 + h] for h in (2 * pair, 2 * pair + 1)
        ]
        out_ref[:, lanes] = (numer / jnp.where(low, halves[0], halves[1])).astype(jnp.bfloat16)


def combine(parts):
    return pl.pallas_call(
        combine_kernel,
        out_shape=jax.ShapeDtypeStruct((parts.shape[1], INNER), jnp.bfloat16),
        in_specs=[VMEM],
        out_specs=VMEM,
        compiler_params=pltpu.CompilerParams(vmem_limit_bytes=8 * 1024 * 1024),
    )(parts)


AXES = ("row", "col")
DEVICES = 256
NX, NY, NZ = 4, 4, 8
SHARE = 0b00100110
REST = 0b11111111 ^ SHARE


def place_of(x, y, z, core):
    return x * 64 + (y // 2) * 32 + z * 4 + (y % 2) * 2 + core


def moved(dx=0, dz=0, dcore=0):
    pairs = []
    for x in range(NX):
        for y in range(NY):
            for z in range(NZ):
                for core in range(2):
                    target = place_of((x + dx) % NX, y, (z + dz) % NZ, (core + dcore) % 2)
                    pairs.append((place_of(x, y, z, core), target))
    return sorted(pairs)


def groups_of(mask):
    found = {}
    for i in range(DEVICES):
        found.setdefault(i & ~mask, []).append(i)
    return list(found.values())


def exchange(value, mask):
    return lax.all_to_all(value, AXES, 0, 0, axis_index_groups=groups_of(mask))


def local(
    latent, gn_gain, gn_bias, w_in, b_in, ln_gain, ln_bias, w_query, w_key, w_value, stale_kv
):
    shared = 8
    with jax.named_scope("keys_z"):
        along_z = [lax.ppermute(stale_kv, AXES, moved(dz=d)) for d in (4, 2, 6)]
    with jax.named_scope("statistics"):
        here = statistics(latent, DEVICES)[:, None, :]
        stats = lax.all_to_all(here, AXES, 0, 0).reshape(DEVICES, 2 * GROUPS)
    with jax.named_scope("keys_x"):
        line = jnp.stack([stale_kv] + along_z)
        parts = [line] + [lax.ppermute(line, AXES, moved(dx=d)) for d in (1, 3, 2)]
    rows, chans = latent.shape
    group = coefficients(stats, rows * (chans // GROUPS), chans)
    scaled = (latent.astype(jnp.float32) - group[0:1]) * group[1:2]
    normed = (scaled * gn_gain + gn_bias).astype(jnp.bfloat16)
    stream = (jnp.dot(normed, w_in, preferred_element_type=jnp.float32) + b_in).astype(jnp.bfloat16)
    wide = stream.astype(jnp.float32)
    token_mean = jnp.mean(wide, axis=-1, keepdims=True)
    token_dev = wide - token_mean
    token_var = jnp.mean(token_dev * token_dev, axis=-1, keepdims=True)
    lnorm = (token_dev * lax.rsqrt(token_var + 1e-05) * ln_gain + ln_bias).astype(jnp.bfloat16)
    query = jnp.dot(lnorm, w_query, preferred_element_type=jnp.float32).astype(jnp.bfloat16)
    query = query * jnp.bfloat16(1.0 / math.sqrt(HEAD_DIM))
    query = jnp.broadcast_to(query[None], (shared, rows, INNER))
    with jax.named_scope("queries"):
        query = exchange(query, SHARE).reshape(shared * latent.shape[0], INNER)
    with jax.named_scope("keys_core"):
        parts = parts + [lax.ppermute(part, AXES, moved(dcore=1)) for part in parts]
    row, col = lax.axis_index("row"), lax.axis_index("col")
    place = ((row & 1) << 2) | (((col >> 2) & 1) << 1) | ((col >> 1) & 1)
    place = place.reshape(1).astype(jnp.int32)
    fresh_kv = jnp.stack(
        [
            jnp.dot(lnorm, w, preferred_element_type=jnp.float32).astype(jnp.bfloat16)
            for w in (w_key, w_value)
        ]
    )
    partial = attend(place, query, fresh_kv, parts)
    with jax.named_scope("partials"):
        attended = combine(exchange(partial, SHARE))
    return (stream, fresh_kv, attended)


def solution(mesh):
    placed = (
        P(AXES, None),
        P(),
        P(),
        P(),
        P(),
        P(),
        P(),
        P(),
        P(),
        P(),
        P(None, AXES, None),
    )
    return jax.shard_map(
        local,
        mesh=mesh,
        in_specs=placed,
        out_specs=(P(AXES, None), P(None, AXES, None), P(AXES, None)),
        check_vma=False,
    )
```

```python
import functools
import math
import jax
import jax.numpy as jnp
from jax import lax
from jax.experimental import pallas as pl
from jax.experimental.pallas import tpu as pltpu
from jax.sharding import PartitionSpec as P

GROUPS = 32
HEADS = 10
HEAD_DIM = 64
INNER = HEADS * HEAD_DIM
VMEM = pl.BlockSpec(memory_space=pltpu.VMEM)
SMEM = pl.BlockSpec(memory_space=pltpu.SMEM)
HBM = pl.BlockSpec(memory_space=pltpu.HBM)
NT = (((1,), (1,)), ((), ()))
ATT_LIMIT = 16 * 1024 * 1024


def member_of(chans):
    width = chans // GROUPS
    first = lax.broadcasted_iota(jnp.int32, (chans, 128), 1) * width
    chan = lax.broadcasted_iota(jnp.int32, (chans, 128), 0)
    inside = (chan >= first) & (chan < first + width)
    return jnp.where(inside, 1.0, 0.0).astype(jnp.bfloat16)


def pieces(value):
    a = value.astype(jnp.bfloat16)
    rest = value - a.astype(jnp.float32)
    b = rest.astype(jnp.bfloat16)
    c = (rest - b.astype(jnp.float32)).astype(jnp.bfloat16)
    return jnp.concatenate([a, b, c], axis=0)


def to_groups(row, member):
    got = jnp.dot(pieces(row), member, preferred_element_type=jnp.float32)
    return got[0:1] + got[1:2] + got[2:3]


def to_channels(row, member):
    got = lax.dot_general(pieces(row), member, NT, preferred_element_type=jnp.float32)
    return got[0:1] + got[1:2] + got[2:3]


def statistics_kernel(x_ref, out_ref):
    rows, chans = x_ref.shape
    entries = rows * (chans // GROUPS)
    member = member_of(chans)
    x = x_ref[...].astype(jnp.float32)
    mean = to_groups(jnp.sum(x, axis=0, keepdims=True), member) * (1.0 / entries)
    off = x - to_channels(mean, member)
    square = to_groups(jnp.sum(off * off, axis=0, keepdims=True), member)
    lane = lax.broadcasted_iota(jnp.int32, (1, 128), 1)
    both = jnp.where(lane < GROUPS, mean, pltpu.roll(square, GROUPS, axis=1))
    out_ref[...] = jnp.broadcast_to(both[:, : 2 * GROUPS], out_ref.shape)


def statistics(x, peers):
    return pl.pallas_call(
        statistics_kernel,
        out_shape=jax.ShapeDtypeStruct((peers, 2 * GROUPS), jnp.float32),
        in_specs=[VMEM],
        out_specs=VMEM,
        compiler_params=pltpu.CompilerParams(vmem_limit_bytes=8 * 1024 * 1024),
    )(x)


def coefficients_kernel(entries, stats_ref, out_ref):
    peers = stats_ref.shape[0]
    means = stats_ref[:, :GROUPS]
    mean = jnp.sum(means, axis=0, keepdims=True) * (1.0 / peers)
    apart = means - mean
    square = jnp.sum(stats_ref[:, GROUPS:] + entries * (apart * apart), axis=0, keepdims=True)
    scale = lax.rsqrt(square * (1.0 / (entries * peers)) + 1e-06)
    rest = jnp.zeros((1, 128 - GROUPS), jnp.float32)
    mean = jnp.concatenate([mean, rest], axis=1)
    scale = jnp.concatenate([scale, rest], axis=1)
    both = lax.dot_general(
        jnp.concatenate([pieces(mean), pieces(scale)], axis=0),
        member_of(out_ref.shape[1]),
        NT,
        preferred_element_type=jnp.float32,
    )
    out_ref[...] = jnp.concatenate(
        [both[at : at + 1] + both[at + 1 : at + 2] + both[at + 2 : at + 3] for at in (0, 3)], axis=0
    )


def coefficients(stats, entries, chans):
    return pl.pallas_call(
        functools.partial(coefficients_kernel, entries),
        out_shape=jax.ShapeDtypeStruct((2, chans), jnp.float32),
        in_specs=[VMEM],
        out_specs=VMEM,
        compiler_params=pltpu.CompilerParams(vmem_limit_bytes=8 * 1024 * 1024),
    )(stats)


def attend_kernel(place_ref, q_ref, fresh_ref, *refs):
    sources, refs = refs[:-7], refs[-7:]
    out_ref, kv_ref, p_ref, more_ref, numer_ref, total_ref, sems = refs
    copies = [
        pltpu.make_async_copy(source, kv_ref.at[i], sems.at[i])
        for i, source in enumerate(sources)
    ]
    for copy in copies:
        copy.start()
    patch = fresh_ref.shape[1]
    rows = q_ref.shape[0]
    count = rows // patch
    place = place_ref[0]
    own = place * patch
    lane = lax.broadcasted_iota(jnp.int32, (1, 128), 1)
    low = lane < HEAD_DIM
    pairs = [slice(at * 128, at * 128 + 128) for at in range(HEADS // 2)]

    def two_heads(part):
        zero = jnp.zeros_like(part)
        return jnp.concatenate([jnp.where(low, part, zero), jnp.where(low, zero, part)], axis=0)

    def with_ones(value):
        return jnp.concatenate([value, jnp.ones((value.shape[0], 128), jnp.bfloat16)], axis=1)

    for pair, lanes in enumerate(pairs):
        score = lax.dot_general(
            two_heads(q_ref[pl.ds(own, patch), lanes]),
            fresh_ref[0, :, lanes],
            NT,
            preferred_element_type=jnp.float32,
        )
        more_ref[pair] = jnp.dot(
            jnp.exp(score).astype(jnp.bfloat16),
            with_ones(fresh_ref[1, :, lanes]),
            preferred_element_type=jnp.float32,
        )
    for copy in copies:
        copy.wait()

    keys = p_ref.shape[1]
    row = lax.broadcasted_iota(jnp.int32, (2 * rows, 1), 0)
    row = jnp.where(row >= rows, row - rows, row)
    is_own = (row >= own) & (row < own + patch)
    totals = jnp.zeros((rows, 128), jnp.float32)
    own_totals = jnp.zeros((patch, 128), jnp.float32)
    step = 128
    for pair, lanes in enumerate(pairs):
        query = two_heads(q_ref[:, lanes])
        key = kv_ref[:, :, 0, :, lanes].reshape(keys, 128)
        value = kv_ref[:, :, 1, :, lanes].reshape(keys, 128)
        for at in range(0, keys, step):
            score = lax.dot_general(
                query, key[at : at + step], NT, preferred_element_type=jnp.float32
            )
            weight = jnp.exp(score)
            if at == 0:
                column = lax.broadcasted_iota(jnp.int32, (1, step), 1)
                weight = jnp.where(is_own & (column < patch), 0.0, weight)
            p_ref[:, at : at + step] = weight.astype(jnp.bfloat16)
        acc = jnp.dot(p_ref[...], with_ones(value), preferred_element_type=jnp.float32)
        numer = jnp.where(low, acc[:rows, :128], acc[rows:, :128])
        out_ref[:, :, lanes] = numer.astype(jnp.bfloat16).reshape(count, patch, 128)
        numer_ref[...] = numer
        more = more_ref[pair]
        mine = numer_ref[pl.ds(own, patch), :] + jnp.where(
            low, more[:patch, :128], more[patch:, :128]
        )
        out_ref[place, :, lanes] = mine.astype(jnp.bfloat16)
        for half in range(2):
            head = 2 * pair + half
            here = (lane == head) | (lane == 16 + head)
            totals = jnp.where(here, acc[half * rows : (half + 1) * rows, 128:], totals)
            own_totals = jnp.where(here, more[half * patch : (half + 1) * patch, 128:], own_totals)

    def coded(total):
        coarse = total.astype(jnp.bfloat16)
        fine = (total - coarse.astype(jnp.float32)).astype(jnp.bfloat16)
        return jnp.where(lane < 16, coarse, fine)

    out_ref[:, :, INNER:] = coded(totals).reshape(count, patch, 128)
    total_ref[...] = totals
    out_ref[place, :, INNER:] = coded(total_ref[pl.ds(own, patch), :] + own_totals)


def attend(place, query, fresh, key_parts):
    rows, patch = query.shape[0], fresh.shape[1]
    keys = sum(p.shape[0] for p in key_parts) * patch
    return pl.pallas_call(
        attend_kernel,
        out_shape=jax.ShapeDtypeStruct((rows // patch, patch, INNER + 128), jnp.bfloat16),
        in_specs=[SMEM, VMEM, VMEM] + [HBM] * len(key_parts),
        out_specs=VMEM,
        scratch_shapes=[
            pltpu.VMEM((len(key_parts),) + key_parts[0].shape, jnp.bfloat16),
            pltpu.VMEM((2 * rows, keys), jnp.bfloat16),
            pltpu.VMEM((HEADS // 2, 2 * patch, 256), jnp.float32),
            pltpu.VMEM((rows, 128), jnp.float32),
            pltpu.VMEM((rows, 128), jnp.float32),
            pltpu.SemaphoreType.DMA((len(key_parts),)),
        ],
        compiler_params=pltpu.CompilerParams(vmem_limit_bytes=ATT_LIMIT),
        cost_estimate=pl.CostEstimate(
            flops=rows * 4 * keys * INNER,
            bytes_accessed=4 * 1024 * 1024,
            transcendentals=rows * keys * HEADS,
        ),
    )(place, query, fresh, *key_parts)


def combine_kernel(parts_ref, out_ref):
    total = jnp.sum(parts_ref[:, :, INNER:].astype(jnp.float32), axis=0)
    low = lax.broadcasted_iota(jnp.int32, (1, 128), 1) < HEAD_DIM
    for pair in range(HEADS // 2):
        lanes = slice(pair * 128, pair * 128 + 128)
        numer = jnp.sum(parts_ref[:, :, lanes].astype(jnp.float32), axis=0)
        halves = [
            total[:, h : h + 1] + total[:, 16 + h : 17 + h] for h in (2 * pair, 2 * pair + 1)
        ]
        out_ref[:, lanes] = (numer / jnp.where(low, halves[0], halves[1])).astype(jnp.bfloat16)


def combine(parts):
    return pl.pallas_call(
        combine_kernel,
        out_shape=jax.ShapeDtypeStruct((parts.shape[1], INNER), jnp.bfloat16),
        in_specs=[VMEM],
        out_specs=VMEM,
        compiler_params=pltpu.CompilerParams(vmem_limit_bytes=8 * 1024 * 1024),
    )(parts)


AXES = ("row", "col")
DEVICES = 256
NX, NY, NZ = 4, 4, 8
SHARE = 0b00100110
REST = 0b11111111 ^ SHARE


def place_of(x, y, z, core):
    return x * 64 + (y // 2) * 32 + z * 4 + (y % 2) * 2 + core


def moved(dx=0, dz=0, dcore=0):
    pairs = []
    for x in range(NX):
        for y in range(NY):
            for z in range(NZ):
                for core in range(2):
                    target = place_of((x + dx) % NX, y, (z + dz) % NZ, (core + dcore) % 2)
                    pairs.append((place_of(x, y, z, core), target))
    return sorted(pairs)


def groups_of(mask):
    found = {}
    for i in range(DEVICES):
        found.setdefault(i & ~mask, []).append(i)
    return list(found.values())


def exchange(value, mask):
    return lax.all_to_all(value, AXES, 0, 0, axis_index_groups=groups_of(mask))


def local(
    latent, gn_gain, gn_bias, w_in, b_in, ln_gain, ln_bias, w_query, w_key, w_value, stale_kv
):
    shared = 8
    with jax.named_scope("keys_z"):
        along_z = [lax.ppermute(stale_kv, AXES, moved(dz=d)) for d in (4, 2, 6)]
    with jax.named_scope("statistics"):
        here = statistics(latent, DEVICES)[:, None, :]
        stats = lax.all_to_all(here, AXES, 0, 0).reshape(DEVICES, 2 * GROUPS)
    with jax.named_scope("keys_x"):
        line = jnp.stack([stale_kv] + along_z)
        parts = [line] + [lax.ppermute(line, AXES, moved(dx=d)) for d in (1, 3, 2)]
    rows, chans = latent.shape
    group = coefficients(stats, rows * (chans // GROUPS), chans)
    scaled = (latent.astype(jnp.float32) - group[0:1]) * group[1:2]
    normed = (scaled * gn_gain + gn_bias).astype(jnp.bfloat16)
    stream = (jnp.dot(normed, w_in, preferred_element_type=jnp.float32) + b_in).astype(jnp.bfloat16)
    wide = stream.astype(jnp.float32)
    token_mean = jnp.mean(wide, axis=-1, keepdims=True)
    token_dev = wide - token_mean
    token_var = jnp.mean(token_dev * token_dev, axis=-1, keepdims=True)
    lnorm = (token_dev * lax.rsqrt(token_var + 1e-05) * ln_gain + ln_bias).astype(jnp.bfloat16)
    query = jnp.dot(lnorm, w_query, preferred_element_type=jnp.float32).astype(jnp.bfloat16)
    query = query * jnp.bfloat16(1.0 / math.sqrt(HEAD_DIM))
    query = jnp.broadcast_to(query[None], (shared, rows, INNER))
    with jax.named_scope("queries"):
        query = exchange(query, SHARE).reshape(shared * latent.shape[0], INNER)
    with jax.named_scope("keys_core"):
        parts[:2] = lax.optimization_barrier(parts[:2])
        parts = parts + [lax.ppermute(part, AXES, moved(dcore=1)) for part in parts]
    row, col = lax.axis_index("row"), lax.axis_index("col")
    place = ((row & 1) << 2) | (((col >> 2) & 1) << 1) | ((col >> 1) & 1)
    place = place.reshape(1).astype(jnp.int32)
    fresh_kv = jnp.stack(
        [
            jnp.dot(lnorm, w, preferred_element_type=jnp.float32).astype(jnp.bfloat16)
            for w in (w_key, w_value)
        ]
    )
    partial = attend(place, query, fresh_kv, parts)
    with jax.named_scope("partials"):
        attended = combine(exchange(partial, SHARE))
    return (stream, fresh_kv, attended)


def solution(mesh):
    placed = (
        P(AXES, None),
        P(),
        P(),
        P(),
        P(),
        P(),
        P(),
        P(),
        P(),
        P(),
        P(None, AXES, None),
    )
    return jax.shard_map(
        local,
        mesh=mesh,
        in_specs=placed,
        out_specs=(P(AXES, None), P(None, AXES, None), P(AXES, None)),
        check_vma=False,
    )
```

```python
import functools
import math
import jax
import jax.numpy as jnp
from jax import lax
from jax.experimental import pallas as pl
from jax.experimental.pallas import tpu as pltpu
from jax.sharding import PartitionSpec as P

GROUPS = 32
HEADS = 10
HEAD_DIM = 64
INNER = HEADS * HEAD_DIM
VMEM = pl.BlockSpec(memory_space=pltpu.VMEM)
SMEM = pl.BlockSpec(memory_space=pltpu.SMEM)
HBM = pl.BlockSpec(memory_space=pltpu.HBM)
NT = (((1,), (1,)), ((), ()))
ATT_LIMIT = 16 * 1024 * 1024


def member_of(chans):
    width = chans // GROUPS
    first = lax.broadcasted_iota(jnp.int32, (chans, 128), 1) * width
    chan = lax.broadcasted_iota(jnp.int32, (chans, 128), 0)
    inside = (chan >= first) & (chan < first + width)
    return jnp.where(inside, 1.0, 0.0).astype(jnp.bfloat16)


def pieces(value):
    a = value.astype(jnp.bfloat16)
    rest = value - a.astype(jnp.float32)
    b = rest.astype(jnp.bfloat16)
    c = (rest - b.astype(jnp.float32)).astype(jnp.bfloat16)
    return jnp.concatenate([a, b, c], axis=0)


def to_groups(row, member):
    got = jnp.dot(pieces(row), member, preferred_element_type=jnp.float32)
    return got[0:1] + got[1:2] + got[2:3]


def to_channels(row, member):
    got = lax.dot_general(pieces(row), member, NT, preferred_element_type=jnp.float32)
    return got[0:1] + got[1:2] + got[2:3]


def statistics_kernel(x_ref, out_ref):
    rows, chans = x_ref.shape
    entries = rows * (chans // GROUPS)
    member = member_of(chans)
    x = x_ref[...].astype(jnp.float32)
    mean = to_groups(jnp.sum(x, axis=0, keepdims=True), member) * (1.0 / entries)
    off = x - to_channels(mean, member)
    square = to_groups(jnp.sum(off * off, axis=0, keepdims=True), member)
    lane = lax.broadcasted_iota(jnp.int32, (1, 128), 1)
    both = jnp.where(lane < GROUPS, mean, pltpu.roll(square, GROUPS, axis=1))
    out_ref[...] = jnp.broadcast_to(both[:, : 2 * GROUPS], out_ref.shape)


def statistics(x, peers):
    return pl.pallas_call(
        statistics_kernel,
        out_shape=jax.ShapeDtypeStruct((peers, 2 * GROUPS), jnp.float32),
        in_specs=[VMEM],
        out_specs=VMEM,
        compiler_params=pltpu.CompilerParams(vmem_limit_bytes=8 * 1024 * 1024),
    )(x)


def coefficients_kernel(entries, stats_ref, mean_ref, scale_ref):
    peers = stats_ref.shape[0]
    means = stats_ref[:, :GROUPS]
    mean = jnp.sum(means, axis=0, keepdims=True) * (1.0 / peers)
    apart = means - mean
    square = jnp.sum(stats_ref[:, GROUPS:] + entries * (apart * apart), axis=0, keepdims=True)
    scale = lax.rsqrt(square * (1.0 / (entries * peers)) + 1e-06)
    rest = jnp.zeros((1, 128 - GROUPS), jnp.float32)
    mean = jnp.concatenate([mean, rest], axis=1)
    scale = jnp.concatenate([scale, rest], axis=1)
    both = lax.dot_general(
        jnp.concatenate([pieces(mean), pieces(scale)], axis=0),
        member_of(mean_ref.shape[0]),
        NT,
        preferred_element_type=jnp.float32,
    )
    for at, ref in ((0, mean_ref), (3, scale_ref)):
        row = both[at : at + 1] + both[at + 1 : at + 2] + both[at + 2 : at + 3]
        ref[...] = row.reshape(ref.shape)


def coefficients(stats, entries, chans):
    return pl.pallas_call(
        functools.partial(coefficients_kernel, entries),
        out_shape=(jax.ShapeDtypeStruct((chans,), jnp.float32),) * 2,
        in_specs=[VMEM],
        out_specs=(VMEM, VMEM),
        compiler_params=pltpu.CompilerParams(vmem_limit_bytes=8 * 1024 * 1024),
    )(stats)


def attend_kernel(place_ref, q_ref, fresh_ref, *refs):
    sources, refs = refs[:-7], refs[-7:]
    out_ref, kv_ref, p_ref, more_ref, numer_ref, total_ref, sems = refs
    copies = [
        pltpu.make_async_copy(source, kv_ref.at[i], sems.at[i])
        for i, source in enumerate(sources)
    ]
    for copy in copies:
        copy.start()
    patch = fresh_ref.shape[1]
    rows = q_ref.shape[0]
    count = rows // patch
    place = place_ref[0]
    own = place * patch
    lane = lax.broadcasted_iota(jnp.int32, (1, 128), 1)
    low = lane < HEAD_DIM
    pairs = [slice(at * 128, at * 128 + 128) for at in range(HEADS // 2)]

    def two_heads(part):
        zero = jnp.zeros_like(part)
        return jnp.concatenate([jnp.where(low, part, zero), jnp.where(low, zero, part)], axis=0)

    def with_ones(value):
        return jnp.concatenate([value, jnp.ones((value.shape[0], 128), jnp.bfloat16)], axis=1)

    for pair, lanes in enumerate(pairs):
        score = lax.dot_general(
            two_heads(q_ref[pl.ds(own, patch), lanes]),
            fresh_ref[0, :, lanes],
            NT,
            preferred_element_type=jnp.float32,
        )
        more_ref[pair] = jnp.dot(
            jnp.exp(score).astype(jnp.bfloat16),
            with_ones(fresh_ref[1, :, lanes]),
            preferred_element_type=jnp.float32,
        )
    for copy in copies:
        copy.wait()

    keys = p_ref.shape[1]
    row = lax.broadcasted_iota(jnp.int32, (2 * rows, 1), 0)
    row = jnp.where(row >= rows, row - rows, row)
    is_own = (row >= own) & (row < own + patch)
    totals = jnp.zeros((rows, 128), jnp.float32)
    own_totals = jnp.zeros((patch, 128), jnp.float32)
    step = 128
    for pair, lanes in enumerate(pairs):
        query = two_heads(q_ref[:, lanes])
        key = kv_ref[:, :, 0, :, lanes].reshape(keys, 128)
        value = kv_ref[:, :, 1, :, lanes].reshape(keys, 128)
        for at in range(0, keys, step):
            score = lax.dot_general(
                query, key[at : at + step], NT, preferred_element_type=jnp.float32
            )
            weight = jnp.exp(score)
            if at == 0:
                column = lax.broadcasted_iota(jnp.int32, (1, step), 1)
                weight = jnp.where(is_own & (column < patch), 0.0, weight)
            p_ref[:, at : at + step] = weight.astype(jnp.bfloat16)
        acc = jnp.dot(p_ref[...], with_ones(value), preferred_element_type=jnp.float32)
        numer = jnp.where(low, acc[:rows, :128], acc[rows:, :128])
        out_ref[:, :, lanes] = numer.astype(jnp.bfloat16).reshape(count, patch, 128)
        numer_ref[...] = numer
        more = more_ref[pair]
        mine = numer_ref[pl.ds(own, patch), :] + jnp.where(
            low, more[:patch, :128], more[patch:, :128]
        )
        out_ref[place, :, lanes] = mine.astype(jnp.bfloat16)
        for half in range(2):
            head = 2 * pair + half
            here = (lane == head) | (lane == 16 + head)
            totals = jnp.where(here, acc[half * rows : (half + 1) * rows, 128:], totals)
            own_totals = jnp.where(here, more[half * patch : (half + 1) * patch, 128:], own_totals)

    def coded(total):
        coarse = total.astype(jnp.bfloat16)
        fine = (total - coarse.astype(jnp.float32)).astype(jnp.bfloat16)
        return jnp.where(lane < 16, coarse, fine)

    out_ref[:, :, INNER:] = coded(totals).reshape(count, patch, 128)
    total_ref[...] = totals
    out_ref[place, :, INNER:] = coded(total_ref[pl.ds(own, patch), :] + own_totals)


def attend(place, query, fresh, key_parts):
    rows, patch = query.shape[0], fresh.shape[1]
    keys = sum(p.shape[0] for p in key_parts) * patch
    return pl.pallas_call(
        attend_kernel,
        out_shape=jax.ShapeDtypeStruct((rows // patch, patch, INNER + 128), jnp.bfloat16),
        in_specs=[SMEM, VMEM, VMEM] + [HBM] * len(key_parts),
        out_specs=VMEM,
        scratch_shapes=[
            pltpu.VMEM((len(key_parts),) + key_parts[0].shape, jnp.bfloat16),
            pltpu.VMEM((2 * rows, keys), jnp.bfloat16),
            pltpu.VMEM((HEADS // 2, 2 * patch, 256), jnp.float32),
            pltpu.VMEM((rows, 128), jnp.float32),
            pltpu.VMEM((rows, 128), jnp.float32),
            pltpu.SemaphoreType.DMA((len(key_parts),)),
        ],
        compiler_params=pltpu.CompilerParams(vmem_limit_bytes=ATT_LIMIT),
        cost_estimate=pl.CostEstimate(
            flops=rows * 4 * keys * INNER,
            bytes_accessed=4 * 1024 * 1024,
            transcendentals=rows * keys * HEADS,
        ),
    )(place, query, fresh, *key_parts)


def combine_kernel(parts_ref, out_ref):
    total = jnp.sum(parts_ref[:, :, INNER:].astype(jnp.float32), axis=0)
    low = lax.broadcasted_iota(jnp.int32, (1, 128), 1) < HEAD_DIM
    for pair in range(HEADS // 2):
        lanes = slice(pair * 128, pair * 128 + 128)
        numer = jnp.sum(parts_ref[:, :, lanes].astype(jnp.float32), axis=0)
        halves = [
            total[:, h : h + 1] + total[:, 16 + h : 17 + h] for h in (2 * pair, 2 * pair + 1)
        ]
        out_ref[:, lanes] = (numer / jnp.where(low, halves[0], halves[1])).astype(jnp.bfloat16)


def combine(parts):
    return pl.pallas_call(
        combine_kernel,
        out_shape=jax.ShapeDtypeStruct((parts.shape[1], INNER), jnp.bfloat16),
        in_specs=[VMEM],
        out_specs=VMEM,
        compiler_params=pltpu.CompilerParams(vmem_limit_bytes=8 * 1024 * 1024),
    )(parts)


AXES = ("row", "col")
DEVICES = 256
NX, NY, NZ = 4, 4, 8
SHARE = 0b00100110
REST = 0b11111111 ^ SHARE


def place_of(x, y, z, core):
    return x * 64 + (y // 2) * 32 + z * 4 + (y % 2) * 2 + core


def moved(dx=0, dz=0, dcore=0):
    pairs = []
    for x in range(NX):
        for y in range(NY):
            for z in range(NZ):
                for core in range(2):
                    target = place_of((x + dx) % NX, y, (z + dz) % NZ, (core + dcore) % 2)
                    pairs.append((place_of(x, y, z, core), target))
    return sorted(pairs)


def groups_of(mask):
    found = {}
    for i in range(DEVICES):
        found.setdefault(i & ~mask, []).append(i)
    return list(found.values())


def exchange(value, mask):
    return lax.all_to_all(value, AXES, 0, 0, axis_index_groups=groups_of(mask))


def local(
    latent, gn_gain, gn_bias, w_in, b_in, ln_gain, ln_bias, w_query, w_key, w_value, stale_kv
):
    shared = 8
    with jax.named_scope("keys_z"):
        along_z = [lax.ppermute(stale_kv, AXES, moved(dz=d)) for d in (4, 2, 6)]
    with jax.named_scope("statistics"):
        here = statistics(latent, DEVICES)[:, None, :]
        stats = lax.all_to_all(here, AXES, 0, 0).reshape(DEVICES, 2 * GROUPS)
    with jax.named_scope("keys_x"):
        line = jnp.stack([stale_kv] + along_z)
        parts = [line] + [lax.ppermute(line, AXES, moved(dx=d)) for d in (1, 3, 2)]
    rows, chans = latent.shape
    mean, scale = coefficients(stats, rows * (chans // GROUPS), chans)
    scaled = (latent.astype(jnp.float32) - mean) * scale
    normed = (scaled * gn_gain + gn_bias).astype(jnp.bfloat16)
    stream = (jnp.dot(normed, w_in, preferred_element_type=jnp.float32) + b_in).astype(jnp.bfloat16)
    wide = stream.astype(jnp.float32)
    token_mean = jnp.mean(wide, axis=-1, keepdims=True)
    token_dev = wide - token_mean
    token_var = jnp.mean(token_dev * token_dev, axis=-1, keepdims=True)
    lnorm = (token_dev * lax.rsqrt(token_var + 1e-05) * ln_gain + ln_bias).astype(jnp.bfloat16)
    query = jnp.dot(lnorm, w_query, preferred_element_type=jnp.float32).astype(jnp.bfloat16)
    query = query * jnp.bfloat16(1.0 / math.sqrt(HEAD_DIM))
    query = jnp.broadcast_to(query[None], (shared, rows, INNER))
    with jax.named_scope("queries"):
        query = exchange(query, SHARE).reshape(shared * latent.shape[0], INNER)
    with jax.named_scope("keys_core"):
        parts[:2] = lax.optimization_barrier(parts[:2])
        parts = parts + [lax.ppermute(part, AXES, moved(dcore=1)) for part in parts]
    row, col = lax.axis_index("row"), lax.axis_index("col")
    place = ((row & 1) << 2) | (((col >> 2) & 1) << 1) | ((col >> 1) & 1)
    place = place.reshape(1).astype(jnp.int32)
    fresh_kv = jnp.stack(
        [
            jnp.dot(lnorm, w, preferred_element_type=jnp.float32).astype(jnp.bfloat16)
            for w in (w_key, w_value)
        ]
    )
    partial = attend(place, query, fresh_kv, parts)
    with jax.named_scope("partials"):
        attended = combine(exchange(partial, SHARE))
    return (stream, fresh_kv, attended)


def solution(mesh):
    placed = (
        P(AXES, None),
        P(),
        P(),
        P(),
        P(),
        P(),
        P(),
        P(),
        P(),
        P(),
        P(None, AXES, None),
    )
    return jax.shard_map(
        local,
        mesh=mesh,
        in_specs=placed,
        out_specs=(P(AXES, None), P(None, AXES, None), P(AXES, None)),
        check_vma=False,
    )
```

```python
import functools
import math
import jax
import jax.numpy as jnp
from jax import lax
from jax.experimental import pallas as pl
from jax.experimental.pallas import tpu as pltpu
from jax.sharding import PartitionSpec as P

GROUPS = 32
HEADS = 10
HEAD_DIM = 64
INNER = HEADS * HEAD_DIM
VMEM = pl.BlockSpec(memory_space=pltpu.VMEM)
SMEM = pl.BlockSpec(memory_space=pltpu.SMEM)
HBM = pl.BlockSpec(memory_space=pltpu.HBM)
NT = (((1,), (1,)), ((), ()))
ATT_LIMIT = 16 * 1024 * 1024


def member_of(chans):
    width = chans // GROUPS
    first = lax.broadcasted_iota(jnp.int32, (chans, 128), 1) * width
    chan = lax.broadcasted_iota(jnp.int32, (chans, 128), 0)
    inside = (chan >= first) & (chan < first + width)
    return jnp.where(inside, 1.0, 0.0).astype(jnp.bfloat16)


def pieces(value):
    a = value.astype(jnp.bfloat16)
    rest = value - a.astype(jnp.float32)
    b = rest.astype(jnp.bfloat16)
    c = (rest - b.astype(jnp.float32)).astype(jnp.bfloat16)
    return jnp.concatenate([a, b, c], axis=0)


def to_groups(row, member):
    got = jnp.dot(pieces(row), member, preferred_element_type=jnp.float32)
    return got[0:1] + got[1:2] + got[2:3]


def to_channels(row, member):
    got = lax.dot_general(pieces(row), member, NT, preferred_element_type=jnp.float32)
    return got[0:1] + got[1:2] + got[2:3]


def statistics_kernel(x_ref, out_ref):
    rows, chans = x_ref.shape
    entries = rows * (chans // GROUPS)
    member = member_of(chans)
    x = x_ref[...].astype(jnp.float32)
    mean = to_groups(jnp.sum(x, axis=0, keepdims=True), member) * (1.0 / entries)
    off = x - to_channels(mean, member)
    square = to_groups(jnp.sum(off * off, axis=0, keepdims=True), member)
    lane = lax.broadcasted_iota(jnp.int32, (1, 128), 1)
    both = jnp.where(lane < GROUPS, mean, pltpu.roll(square, GROUPS, axis=1))
    out_ref[...] = jnp.broadcast_to(both[:, : 2 * GROUPS], out_ref.shape)


def statistics(x, peers):
    return pl.pallas_call(
        statistics_kernel,
        out_shape=jax.ShapeDtypeStruct((peers, 2 * GROUPS), jnp.float32),
        in_specs=[VMEM],
        out_specs=VMEM,
        compiler_params=pltpu.CompilerParams(vmem_limit_bytes=8 * 1024 * 1024),
    )(x)


def coefficients_kernel(entries, stats_ref, mean_ref, scale_ref):
    peers = stats_ref.shape[0]
    means = stats_ref[:, :GROUPS]
    mean = jnp.sum(means, axis=0, keepdims=True) * (1.0 / peers)
    apart = means - mean
    square = jnp.sum(stats_ref[:, GROUPS:] + entries * (apart * apart), axis=0, keepdims=True)
    scale = lax.rsqrt(square * (1.0 / (entries * peers)) + 1e-06)
    rest = jnp.zeros((1, 128 - GROUPS), jnp.float32)
    mean = jnp.concatenate([mean, rest], axis=1)
    scale = jnp.concatenate([scale, rest], axis=1)
    both = lax.dot_general(
        jnp.concatenate([pieces(mean), pieces(scale)], axis=0),
        member_of(mean_ref.shape[0]),
        NT,
        preferred_element_type=jnp.float32,
    )
    for at, ref in ((0, mean_ref), (3, scale_ref)):
        row = both[at : at + 1] + both[at + 1 : at + 2] + both[at + 2 : at + 3]
        ref[...] = row.reshape(ref.shape)


def coefficients(stats, entries, chans):
    return pl.pallas_call(
        functools.partial(coefficients_kernel, entries),
        out_shape=(jax.ShapeDtypeStruct((chans,), jnp.float32),) * 2,
        in_specs=[VMEM],
        out_specs=(VMEM, VMEM),
        compiler_params=pltpu.CompilerParams(vmem_limit_bytes=8 * 1024 * 1024),
    )(stats)


def attend_kernel(place_ref, q_ref, fresh_ref, *refs):
    sources, refs = refs[:-7], refs[-7:]
    out_ref, kv_ref, p_ref, more_ref, numer_ref, total_ref, sems = refs
    copies = [
        pltpu.make_async_copy(source, kv_ref.at[i], sems.at[i])
        for i, source in enumerate(sources)
    ]
    for copy in copies:
        copy.start()
    patch = fresh_ref.shape[1]
    rows = q_ref.shape[0]
    count = rows // patch
    place = place_ref[0]
    own = place * patch
    lane = lax.broadcasted_iota(jnp.int32, (1, 128), 1)
    low = lane < HEAD_DIM
    pairs = [slice(at * 128, at * 128 + 128) for at in range(HEADS // 2)]

    def two_heads(part):
        zero = jnp.zeros_like(part)
        return jnp.concatenate([jnp.where(low, part, zero), jnp.where(low, zero, part)], axis=0)

    def with_ones(value):
        return jnp.concatenate([value, jnp.ones((value.shape[0], 128), jnp.bfloat16)], axis=1)

    for pair, lanes in enumerate(pairs):
        score = lax.dot_general(
            two_heads(q_ref[pl.ds(own, patch), lanes]),
            fresh_ref[0, :, lanes],
            NT,
            preferred_element_type=jnp.float32,
        )
        more_ref[pair] = jnp.dot(
            jnp.exp(score).astype(jnp.bfloat16),
            with_ones(fresh_ref[1, :, lanes]),
            preferred_element_type=jnp.float32,
        )
    for copy in copies:
        copy.wait()

    keys = p_ref.shape[2]
    row = lax.broadcasted_iota(jnp.int32, (2 * rows, 1), 0)
    row = jnp.where(row >= rows, row - rows, row)
    is_own = (row >= own) & (row < own + patch)
    totals = jnp.zeros((rows, 128), jnp.float32)
    own_totals = jnp.zeros((patch, 128), jnp.float32)
    step = 256
    for pair, lanes in enumerate(pairs):
        query = two_heads(q_ref[:, lanes])
        key = kv_ref[:, :, 0, :, lanes].reshape(keys, 128)
        value = kv_ref[:, :, 1, :, lanes].reshape(keys, 128)
        for at in range(0, keys, step):
            score = lax.dot_general(
                query, key[at : at + step], NT, preferred_element_type=jnp.float32
            )
            weight = jnp.exp(score)
            if at == 0:
                column = lax.broadcasted_iota(jnp.int32, (1, step), 1)
                weight = jnp.where(is_own & (column < patch), 0.0, weight)
            p_ref[pair % 2, :, at : at + step] = weight.astype(jnp.bfloat16)
        acc = jnp.dot(p_ref[pair % 2], with_ones(value), preferred_element_type=jnp.float32)
        numer = jnp.where(low, acc[:rows, :128], acc[rows:, :128])
        out_ref[:, :, lanes] = numer.astype(jnp.bfloat16).reshape(count, patch, 128)
        numer_ref[...] = numer
        more = more_ref[pair]
        mine = numer_ref[pl.ds(own, patch), :] + jnp.where(
            low, more[:patch, :128], more[patch:, :128]
        )
        out_ref[place, :, lanes] = mine.astype(jnp.bfloat16)
        for half in range(2):
            head = 2 * pair + half
            here = (lane == head) | (lane == 16 + head)
            totals = jnp.where(here, acc[half * rows : (half + 1) * rows, 128:], totals)
            own_totals = jnp.where(here, more[half * patch : (half + 1) * patch, 128:], own_totals)

    def coded(total):
        coarse = total.astype(jnp.bfloat16)
        fine = (total - coarse.astype(jnp.float32)).astype(jnp.bfloat16)
        return jnp.where(lane < 16, coarse, fine)

    out_ref[:, :, INNER:] = coded(totals).reshape(count, patch, 128)
    total_ref[...] = totals
    out_ref[place, :, INNER:] = coded(total_ref[pl.ds(own, patch), :] + own_totals)


def attend(place, query, fresh, key_parts):
    rows, patch = query.shape[0], fresh.shape[1]
    keys = sum(p.shape[0] for p in key_parts) * patch
    return pl.pallas_call(
        attend_kernel,
        out_shape=jax.ShapeDtypeStruct((rows // patch, patch, INNER + 128), jnp.bfloat16),
        in_specs=[SMEM, VMEM, VMEM] + [HBM] * len(key_parts),
        out_specs=VMEM,
        scratch_shapes=[
            pltpu.VMEM((len(key_parts),) + key_parts[0].shape, jnp.bfloat16),
            pltpu.VMEM((2, 2 * rows, keys), jnp.bfloat16),
            pltpu.VMEM((HEADS // 2, 2 * patch, 256), jnp.float32),
            pltpu.VMEM((rows, 128), jnp.float32),
            pltpu.VMEM((rows, 128), jnp.float32),
            pltpu.SemaphoreType.DMA((len(key_parts),)),
        ],
        compiler_params=pltpu.CompilerParams(vmem_limit_bytes=ATT_LIMIT),
        cost_estimate=pl.CostEstimate(
            flops=rows * 4 * keys * INNER,
            bytes_accessed=4 * 1024 * 1024,
            transcendentals=rows * keys * HEADS,
        ),
    )(place, query, fresh, *key_parts)


def combine_kernel(parts_ref, out_ref):
    total = jnp.sum(parts_ref[:, :, INNER:].astype(jnp.float32), axis=0)
    low = lax.broadcasted_iota(jnp.int32, (1, 128), 1) < HEAD_DIM
    for pair in range(HEADS // 2):
        lanes = slice(pair * 128, pair * 128 + 128)
        numer = jnp.sum(parts_ref[:, :, lanes].astype(jnp.float32), axis=0)
        halves = [
            total[:, h : h + 1] + total[:, 16 + h : 17 + h] for h in (2 * pair, 2 * pair + 1)
        ]
        out_ref[:, lanes] = (numer / jnp.where(low, halves[0], halves[1])).astype(jnp.bfloat16)


def combine(parts):
    return pl.pallas_call(
        combine_kernel,
        out_shape=jax.ShapeDtypeStruct((parts.shape[1], INNER), jnp.bfloat16),
        in_specs=[VMEM],
        out_specs=VMEM,
        compiler_params=pltpu.CompilerParams(vmem_limit_bytes=8 * 1024 * 1024),
    )(parts)


AXES = ("row", "col")
DEVICES = 256
NX, NY, NZ = 4, 4, 8
SHARE = 0b00100110
REST = 0b11111111 ^ SHARE


def place_of(x, y, z, core):
    return x * 64 + (y // 2) * 32 + z * 4 + (y % 2) * 2 + core


def moved(dx=0, dz=0, dcore=0):
    pairs = []
    for x in range(NX):
        for y in range(NY):
            for z in range(NZ):
                for core in range(2):
                    target = place_of((x + dx) % NX, y, (z + dz) % NZ, (core + dcore) % 2)
                    pairs.append((place_of(x, y, z, core), target))
    return sorted(pairs)


def groups_of(mask):
    found = {}
    for i in range(DEVICES):
        found.setdefault(i & ~mask, []).append(i)
    return list(found.values())


def exchange(value, mask):
    return lax.all_to_all(value, AXES, 0, 0, axis_index_groups=groups_of(mask))


def local(
    latent, gn_gain, gn_bias, w_in, b_in, ln_gain, ln_bias, w_query, w_key, w_value, stale_kv
):
    shared = 8
    with jax.named_scope("keys_z"):
        along_z = [lax.ppermute(stale_kv, AXES, moved(dz=d)) for d in (4, 2, 6)]
    with jax.named_scope("statistics"):
        here = statistics(latent, DEVICES)[:, None, :]
        stats = lax.all_to_all(here, AXES, 0, 0).reshape(DEVICES, 2 * GROUPS)
    with jax.named_scope("keys_x"):
        line = jnp.stack([stale_kv] + along_z)
        parts = [line] + [lax.ppermute(line, AXES, moved(dx=d)) for d in (1, 3, 2)]
    rows, chans = latent.shape
    mean, scale = coefficients(stats, rows * (chans // GROUPS), chans)
    scaled = (latent.astype(jnp.float32) - mean) * scale
    normed = (scaled * gn_gain + gn_bias).astype(jnp.bfloat16)
    stream = (jnp.dot(normed, w_in, preferred_element_type=jnp.float32) + b_in).astype(jnp.bfloat16)
    wide = stream.astype(jnp.float32)
    token_mean = jnp.mean(wide, axis=-1, keepdims=True)
    token_dev = wide - token_mean
    token_var = jnp.mean(token_dev * token_dev, axis=-1, keepdims=True)
    lnorm = (token_dev * lax.rsqrt(token_var + 1e-05) * ln_gain + ln_bias).astype(jnp.bfloat16)
    query = jnp.dot(lnorm, w_query, preferred_element_type=jnp.float32).astype(jnp.bfloat16)
    query = query * jnp.bfloat16(1.0 / math.sqrt(HEAD_DIM))
    query = jnp.broadcast_to(query[None], (shared, rows, INNER))
    with jax.named_scope("queries"):
        query = exchange(query, SHARE).reshape(shared * latent.shape[0], INNER)
    with jax.named_scope("keys_core"):
        parts[:2] = lax.optimization_barrier(parts[:2])
        parts = parts + [lax.ppermute(part, AXES, moved(dcore=1)) for part in parts]
    row, col = lax.axis_index("row"), lax.axis_index("col")
    place = ((row & 1) << 2) | (((col >> 2) & 1) << 1) | ((col >> 1) & 1)
    place = place.reshape(1).astype(jnp.int32)
    fresh_kv = jnp.stack(
        [
            jnp.dot(lnorm, w, preferred_element_type=jnp.float32).astype(jnp.bfloat16)
            for w in (w_key, w_value)
        ]
    )
    partial = attend(place, query, fresh_kv, parts)
    with jax.named_scope("partials"):
        attended = combine(exchange(partial, SHARE))
    return (stream, fresh_kv, attended)


def solution(mesh):
    placed = (
        P(AXES, None),
        P(),
        P(),
        P(),
        P(),
        P(),
        P(),
        P(),
        P(),
        P(),
        P(None, AXES, None),
    )
    return jax.shard_map(
        local,
        mesh=mesh,
        in_specs=placed,
        out_specs=(P(AXES, None), P(None, AXES, None), P(AXES, None)),
        check_vma=False,
    )
```
